32 devices in a mesh: groups: 2 (over y), wide: 4 (over z), narrow: 2 (over x), sub: 2 (over core).
Axes of the slice: x: 2, y: 2, z: 4, core: 2. Of those that a mesh axis runs over, the one named last changes fastest.
Arguments:
- features: bfloat16 [8192, 96], P(('groups', 'wide', 'narrow', 'sub')), parts along dimension 0, may hold values from -6 to 6
- cotangent: bfloat16 [8192, 96], P(('groups', 'wide', 'narrow', 'sub')), parts along dimension 0, may hold values from -6 to 6
- keys: int32 [8192], P(('groups', 'wide', 'narrow', 'sub')), parts along dimension 0, may hold values from 0 to 8191, as said below
- weight: bfloat16 [27, 96, 96], replicated, may hold values from -0.125 to 0.125
Outputs:
- out_rows: bfloat16 [8192, 96], P(('groups', 'wide', 'narrow', 'sub')), parts along dimension 0
- grad_rows: bfloat16 [8192, 96], P(('groups', 'wide', 'narrow', 'sub')), parts along dimension 0
- weight_grad: float32 [497664], P(('groups', 'wide', 'narrow', 'sub')), parts along dimension 0
The draws below stay inside these ranges and needn't reach their ends.
There are 2 independent parts, one for each index of `groups`. The reference program is written for one: setup_inputs(seed, part) draws one part's arguments, and reference() takes and returns one part's arrays. A program takes and returns all parts, laid end to end along the dimension named above; an argument that names none is the same for every part. Nothing has to cross between parts.
Inputs may be any that keep to these rules, and one draw needn't show every extreme that they name: Keys are distinct and ascend on each device; key // 512 names a brick piece whose sub index equals the holding device's sub index; one device holds at most 64 keys of one brick piece, and for each sub index one brick piece gets exactly 64 keys from every device of that sub index.
All inputs are finite; a program needn't handle non-finite values.
Results may differ from the reference program's by a relative error of at most 0.001.
Values may be sent and summed in bfloat16 or wider, within the bound.
A program may use at most 64 MiB of HBM per device.

```python
import jax
import jax.numpy as jnp
from jax import lax

C = 96
TAPS = 27
EDGE = 16
DEPTH = 4
ROWS_DEV = 256
HALF = 2
CELLS = 512
DEVS = 16
CAP = 64
ROWS = 4096
N_WIDE = 4
N_NARROW = 2
N_SUB = 2


def draw_keys(key, part):
    owners = N_WIDE * N_NARROW
    sub_count = N_SUB
    device_count = owners * sub_count
    key_busy, key_order, key_split, key_cells = jax.random.split(key, 4)
    busy = jax.random.randint(key_busy, (sub_count,), 0, owners)
    sources = jnp.arange(device_count)
    sub_of = sources % sub_count
    orders = jax.vmap(lambda k: jax.random.permutation(k, owners))(jax.random.split(key_order, device_count))
    busy_col = busy[sub_of][:, None]
    leading = orders[:, :1]
    orders = jnp.where(orders == busy_col, leading, orders)
    orders = orders.at[:, 0].set(busy_col[:, 0])
    pair_split = jax.random.randint(key_split, (device_count, owners // 2), 0, CAP + 1)
    pair_split = pair_split.at[:, 0].set(CAP)
    by_place = jnp.stack([pair_split, CAP - pair_split], axis=2).reshape(device_count, owners)
    counts = jnp.zeros((device_count, owners), jnp.int32).at[sources[:, None], orders].set(by_place)
    cell_orders = jax.vmap(lambda k: jax.random.permutation(k, CELLS))(jax.random.split(key_cells, device_count))
    owner_ids = jnp.arange(owners)[None, :] * sub_count + sub_of[:, None]
    slot_index = (sources // sub_count)[:, None, None] * CAP + jnp.arange(CAP)[None, None, :]
    chosen = cell_orders[owner_ids[:, :, None], slot_index]
    is_live = jnp.arange(CAP)[None, None, :] < counts[:, :, None]
    ceiling = device_count * CELLS
    values_all = jnp.where(is_live, owner_ids[:, :, None] * CELLS + chosen, ceiling)
    values_all = jnp.sort(values_all.reshape(device_count, owners * CAP), axis=1)[:, :ROWS_DEV]
    return values_all.reshape(-1).astype(jnp.int32)


def block_levels(stream_key, extent, cuts, low, top_value):
    loudness, own = 1.0, jax.random.fold_in(stream_key, 6)
    for position, shards_of in cuts:
        heights = jnp.exp(jax.random.uniform(jax.random.fold_in(own, position), (shards_of,), jnp.float32, low / len(cuts), top_value / len(cuts)))
        loudness = loudness * jnp.repeat(heights, extent[position] // shards_of).reshape([-1 if axis == position else 1 for axis in range(len(extent))])
    return loudness


def noise(own_key, dims, spread, reach, cuts=(), kind=jnp.bfloat16):
    array = spread * jax.random.normal(own_key, dims, jnp.float32)
    if cuts:
        array = array * block_levels(own_key, dims, cuts, -0.22, 0.18)
    return jnp.clip(array, -reach, reach).astype(kind)


def setup_inputs(seed: int = 0, part: int = 0) -> dict:
    arg_keys = jax.random.split(jax.random.key(seed), 5)
    part_keys = jax.random.split(jax.random.fold_in(arg_keys[4], part), 5)
    return {
        "features": noise(part_keys[0], (ROWS, C), 1.0, 6.0, ((0, 16),)),
        "cotangent": noise(part_keys[1], (ROWS, C), 1.0, 6.0, ((0, 16),)),
        "keys": draw_keys(jax.random.fold_in(jax.random.fold_in(arg_keys[4], part), 71), part),
        "weight": noise(arg_keys[3], (TAPS, C, C), (TAPS * C) ** -0.5, 0.125),
    }


def local_pass(patch, weight):
    chan_count = weight.shape[1]
    fields = patch[..., :chan_count]
    back_field = patch[..., chan_count:]
    centre = back_field[1:-1, 1:-1, 1:-1].reshape(-1, chan_count)
    forward = jnp.zeros((CELLS, chan_count), jnp.float32)
    backward = jnp.zeros((CELLS, chan_count), jnp.float32)
    pieces = []
    for tap_index in range(TAPS):
        step_x = tap_index // 9 - 1
        step_y = tap_index // 3 % 3 - 1
        step_z = tap_index % 3 - 1
        shifted = fields[1 + step_x:1 + step_x + EDGE, 1 + step_y:1 + step_y + EDGE, 1 + step_z:1 + step_z + HALF].reshape(-1, chan_count)
        mirrored = back_field[1 - step_x:1 - step_x + EDGE, 1 - step_y:1 - step_y + EDGE, 1 - step_z:1 - step_z + HALF].reshape(-1, chan_count)
        forward = forward + jnp.dot(shifted, weight[tap_index], preferred_element_type=jnp.float32)
        backward = backward + jnp.dot(mirrored, weight[tap_index].T, preferred_element_type=jnp.float32)
        pieces.append(jnp.dot(shifted.T, centre, preferred_element_type=jnp.float32))
    return (forward.astype(jnp.bfloat16), backward.astype(jnp.bfloat16), jnp.stack(pieces))

def reference(features, cotangent, keys, weight):
    chan_count = features.shape[1]
    owner_id = keys // CELLS
    cell_id = keys % CELLS
    sub_id = owner_id % N_SUB
    narrow_id = owner_id // N_SUB % N_NARROW
    wide_id = owner_id // (N_SUB * N_NARROW)
    along_x = EDGE * narrow_id + cell_id // (EDGE * HALF)
    along_y = EDGE * wide_id + cell_id // HALF % EDGE
    along_z = HALF * sub_id + cell_id % HALF
    payload = jnp.concatenate([features, cotangent], axis=1)
    volume = jnp.zeros((EDGE * N_NARROW + 2, EDGE * N_WIDE + 2, DEPTH + 2, 2 * chan_count), jnp.bfloat16)
    volume = volume.at[along_x + 1, along_y + 1, along_z + 1].set(payload)

    def one_piece(index):
        piece_sub = index % N_SUB
        piece_narrow = index // N_SUB % N_NARROW
        piece_wide = index // (N_SUB * N_NARROW)
        starts = (EDGE * piece_narrow, EDGE * piece_wide, HALF * piece_sub, jnp.int32(0) * index)
        starts = tuple((s.astype(jnp.int32) for s in starts))
        patch = lax.dynamic_slice(volume, starts, (EDGE + 2, EDGE + 2, HALF + 2, 2 * chan_count))
        return local_pass(patch, weight)
    results = lax.map(one_piece, jnp.arange(DEVS, dtype=jnp.int32))
    outputs = results[0].reshape(-1, chan_count)[keys]
    gradient = results[1].reshape(-1, chan_count)[keys]
    factor = jnp.float32(1.0) / jnp.sqrt(jnp.float32(ROWS))
    weight_grad = lax.optimization_barrier(jnp.sum(results[2], axis=0)).reshape(-1) * factor
    return (outputs, gradient, weight_grad)
```

```python
import functools

import jax
import jax.numpy as jnp
from jax import lax
from jax.experimental import pallas as pl
from jax.experimental.pallas import tpu as pltpu
from jax.sharding import PartitionSpec as P

EDGE = 16
DEPTH = 4
LANES = 128
F32, BF16 = jnp.float32, jnp.bfloat16


def window_kernel(
    dims, feat_ref, cot_ref, keys_ref, weight_ref, out_ref, grad_ref, wgrad_ref,
    held, slots, x_field, g_field, x_near, g_near, taps, mask, forward, backward,
    picked, returned, terms, send_sem, recv_sem, reply_send, reply_recv,
):
    wide_n, narrow_n, sub_n, rows, chan, cap, shard = dims
    owners = wide_n * narrow_n
    slot_n = owners * cap
    half = DEPTH // sub_n
    cells = EDGE * EDGE * half
    w, n, s = lax.axis_index("wide"), lax.axis_index("narrow"), lax.axis_index("sub")
    me = w * narrow_n + n

    def number(wi, ni, si):
        return (wi * narrow_n + ni) * sub_n + si

    def place(wi, ni, si):
        return {"wide": wi, "narrow": ni, "sub": si}

    barrier = pltpu.get_barrier_semaphore()
    for delta in range(1, owners):
        peer = lax.rem(me + delta, owners)
        pl.semaphore_signal(
            barrier, inc=1, device_id=place(peer // narrow_n, peer % narrow_n, s),
            device_id_type=pl.DeviceIdType.MESH,
        )
    pl.semaphore_signal(
        barrier, inc=1, device_id=place(w, n, 1 - s), device_id_type=pl.DeviceIdType.MESH
    )

    keys = keys_ref[...]
    target = lax.shift_right_logical(keys, (cells * sub_n).bit_length() - 1)
    local = keys & (cells - 1)
    cell = (local >> 5) * 32 + (local & 1) * EDGE + ((local >> 1) & (EDGE - 1))
    first = jnp.zeros_like(keys)
    for o in range(1, owners):
        before = jnp.sum((target < o).astype(F32), axis=1, keepdims=True).astype(jnp.int32)
        first = jnp.where(target == o, before, first)
    slot = target * cap + lax.broadcasted_iota(jnp.int32, keys.shape, 1) - first
    cell1 = cell + 1
    line = lax.broadcasted_iota(jnp.int32, (LANES, rows), 0)
    digits = jnp.where(line == 0, slot >> 4, 0)
    digits = jnp.where(line == 1, slot & 15, digits)
    digits = jnp.where(line == chan, cell1 >> 4, digits)
    digits = jnp.where(line == chan + 1, cell1 & 15, digits)
    digits = digits.astype(F32).astype(BF16)
    eye = (
        lax.broadcasted_iota(jnp.int32, (rows, rows), 0)
        == lax.broadcasted_iota(jnp.int32, (rows, rows), 1)
    )
    eye = jnp.where(eye, 1.0, 0.0).astype(BF16)
    column = lax.dot_general(eye, digits, (((1,), (1,)), ((), ())), preferred_element_type=F32)
    mine = number(w, n, s)
    held[mine, 0:rows, 0:LANES] = column.astype(BF16)
    held[mine, 0:rows, LANES : 2 * LANES] = jnp.zeros((rows, LANES), BF16)
    held[mine, 0:rows, 0:chan] = feat_ref[...]
    held[mine, 0:rows, LANES : LANES + chan] = cot_ref[...]
    held[mine, rows : rows + 16, :] = digits[0:16]

    pl.semaphore_wait(barrier, owners)

    def block_copy(block, kind, target_place):
        return pltpu.make_async_remote_copy(
            src_ref=held.at[block], dst_ref=held.at[block],
            send_sem=send_sem.at[block, kind], recv_sem=recv_sem.at[block],
            device_id=target_place, device_id_type=pl.DeviceIdType.MESH,
        )

    up, down = place(w + 1, n, s), place(w - 1, n, s)
    across, sibling = place(w, 1 - n, s), place(w, n, 1 - s)

    @pl.when(w + 1 < wide_n)
    def _():
        block_copy(mine, 0, up).start()

    @pl.when(w >= 1)
    def _():
        block_copy(mine, 1, down).start()

    block_copy(mine, 2, across).start()
    block_copy(mine, 3, sibling).start()

    def clear(i, carry):
        x_field[i] = jnp.zeros(x_field.shape[1:], F32)
        g_field[i] = jnp.zeros(g_field.shape[1:], F32)
        return carry

    lax.fori_loop(0, x_field.shape[0], clear, 0)
    taps[...] = jnp.zeros(taps.shape, BF16)
    for t in range(27):
        taps[t, 0:chan, 0:chan] = weight_ref[t]

    def crossed(distance):
        def arrive(wi):
            block = number(wi, 1 - n, s)
            block_copy(block, 2, across).wait_recv()
            block_copy(block, 3, sibling).start()

        if distance == 0:
            arrive(w)
            return

        @pl.when(w >= distance)
        def _():
            arrive(w - distance)

        @pl.when(w + distance < wide_n)
        def _():
            arrive(w + distance)

    for d in range(1, wide_n):

        @pl.when(w >= d)
        def _():
            block = number(w - d, n, s)
            block_copy(block, 0, up).wait_recv()

            @pl.when(w + 1 < wide_n)
            def _():
                block_copy(block, 0, up).start()

            block_copy(block, 2, across).start()
            block_copy(block, 3, sibling).start()

        @pl.when(w + d < wide_n)
        def _():
            block = number(w + d, n, s)
            block_copy(block, 1, down).wait_recv()

            @pl.when(w >= 1)
            def _():
                block_copy(block, 1, down).start()

            block_copy(block, 2, across).start()
            block_copy(block, 3, sibling).start()

        crossed(d - 1)
    crossed(wide_n - 1)

    for o in range(owners):
        block_copy(o * sub_n + 1 - s, 3, sibling).wait_recv()

    for wi in range(wide_n):
        block = number(wi, n, s)

        @pl.when(jnp.logical_and(wi <= w, w + 1 < wide_n))
        def _():
            block_copy(block, 0, up).wait_send()

        @pl.when(jnp.logical_and(wi >= w, w >= 1))
        def _():
            block_copy(block, 1, down).wait_send()

        block_copy(block, 2, across).wait_send()
        for ni in range(narrow_n):
            block_copy(number(wi, ni, s), 3, sibling).wait_send()

    def slot_mask(block):
        lines = held[block, rows : rows + 16, :].astype(F32)
        slot_of = lines[0:1] * 16.0 + lines[1:2]
        order = lax.broadcasted_iota(jnp.int32, (slot_n, rows), 0).astype(F32)
        return jnp.where(order == slot_of, 1.0, 0.0).astype(BF16)

    def to_slots(block, carry):
        filled = jnp.dot(slot_mask(block), held[block, 0:rows, :], preferred_element_type=F32)
        source = block // sub_n
        slots[block % sub_n, :, source] = filled.astype(BF16).reshape(owners, cap, 2 * LANES)
        return carry

    lax.fori_loop(0, owners * sub_n, to_slots, 0)

    row_of = lax.broadcasted_iota(jnp.int32, (16, 2 * LANES), 0)
    lane_of = lax.broadcasted_iota(jnp.int32, (16, 2 * LANES), 1)
    chooser = jnp.where(lane_of == chan, 16.0, jnp.where(lane_of == chan + 1, 1.0, 0.0))
    chooser = jnp.where(row_of == 0, chooser, 0.0).astype(BF16)

    def cell_mask(block):
        rows_in = slots[block % sub_n, block // sub_n].reshape(slot_n, 2 * LANES)
        cell_of = lax.dot_general(
            chooser, rows_in, (((1,), (1,)), ((), ())), preferred_element_type=F32
        )[0:1]
        order = lax.broadcasted_iota(jnp.int32, (cells, slot_n), 0).astype(F32) + 1.0
        return jnp.where(order == cell_of, 1.0, 0.0).astype(BF16), rows_in

    def to_field(block, carry):
        ones, rows_in = cell_mask(block)
        dense = jnp.dot(ones, rows_in, preferred_element_type=F32)
        dense = dense.reshape(EDGE, half, EDGE, 2 * LANES)
        owner = block // sub_n
        at = (
            pl.ds(1 + EDGE * (owner % narrow_n), EDGE),
            pl.ds(1 + half * (block % sub_n), half),
            pl.ds(pl.multiple_of(EDGE + EDGE * (owner // narrow_n), EDGE), EDGE),
        )
        x_field[at] = dense[..., 0:LANES]
        g_field[at] = dense[..., LANES : 2 * LANES]
        return carry

    lax.fori_loop(0, owners * sub_n, to_field, 0)
    mask[...] = cell_mask(mine)[0]

    wide_at = pl.ds(pl.multiple_of(EDGE * w, EDGE), 3 * EDGE)

    def near(i, carry):
        for k in range(half + 2):
            x_line = x_field[EDGE * n + i, half * s + k, wide_at, :]
            g_line = g_field[EDGE * n + i, half * s + k, wide_at, :]
            for j in range(3):
                begin = EDGE - 1 + j
                x_near[j, i, k] = x_line[begin : begin + EDGE].astype(BF16)
                g_near[j, i, k] = g_line[begin : begin + EDGE].astype(BF16)
        return carry

    lax.fori_loop(0, EDGE + 2, near, 0)

    forward[...] = jnp.zeros(forward.shape, F32)
    backward[...] = jnp.zeros(backward.shape, F32)

    def conv(group, carry):
        i, j = group // 3, group % 3
        ahead = jnp.concatenate(
            [x_near[j, pl.ds(i, EDGE), k : k + half].reshape(cells, LANES) for k in range(3)],
            axis=1,
        )
        behind = [
            g_near[2 - j, pl.ds(2 - i, EDGE), 2 - k : 2 - k + half].reshape(cells, LANES)
            for k in range(3)
        ]
        forward[...] += jnp.dot(
            ahead, taps[pl.ds(3 * group, 3)].reshape(3 * LANES, LANES), preferred_element_type=F32
        )
        total = backward[...]
        for k in range(3):
            total += lax.dot_general(
                behind[k], taps[3 * group + k], (((1,), (1,)), ((), ())),
                preferred_element_type=F32,
            )
        backward[...] = total
        return carry

    lax.fori_loop(0, 9, conv, 0)

    reply = jnp.concatenate([forward[...].astype(BF16), backward[...].astype(BF16)], axis=1)
    rows_out = lax.dot_general(
        mask[...], reply, (((0,), (0,)), ((), ())), preferred_element_type=F32
    ).astype(BF16)
    picked[...] = rows_out.reshape(owners, cap, 2 * LANES)

    def reply_copy(delta):
        peer = lax.rem(me + delta, owners)
        return pltpu.make_async_remote_copy(
            src_ref=picked.at[peer], dst_ref=returned.at[me],
            send_sem=reply_send.at[delta], recv_sem=reply_recv.at[delta],
            device_id=place(peer // narrow_n, peer % narrow_n, s),
            device_id_type=pl.DeviceIdType.MESH,
        )

    def reply_arrival(delta):
        peer = lax.rem(me + owners - delta, owners)
        return pltpu.make_async_remote_copy(
            src_ref=picked.at[peer], dst_ref=returned.at[peer],
            send_sem=reply_send.at[delta], recv_sem=reply_recv.at[delta],
            device_id=place(peer // narrow_n, peer % narrow_n, s),
            device_id_type=pl.DeviceIdType.MESH,
        )

    for delta in range(1, owners):
        reply_copy(delta).start()
    returned[me] = picked[me]

    begin = mine * shard
    tap0 = begin // chan
    whole = EDGE * wide_n
    terms[...] = jnp.zeros(terms.shape, F32)
    steps = []
    for m in range(3):
        t = jnp.minimum(tap0 + m, 26)
        steps.append((t // 9, t // 3 % 3, t % 3))

    def gather(i, carry):
        right = []
        for a, b, c in steps:
            right.append(
                jnp.concatenate(
                    [
                        x_field[i + a, c + k, pl.ds(EDGE - 1 + b, whole), :].astype(BF16)
                        for k in range(DEPTH)
                    ],
                    axis=0,
                )
            )
        left = jnp.concatenate(
            [g_field[1 + i, 1 + k, EDGE : EDGE + whole, :].astype(BF16) for k in range(DEPTH)],
            axis=0,
        )
        terms[...] += lax.dot_general(
            left, jnp.concatenate(right, axis=1), (((0,), (0,)), ((), ())),
            preferred_element_type=F32,
        )
        return carry

    lax.fori_loop(0, EDGE * narrow_n, gather, 0)
    total_rows = rows * owners * sub_n
    factor = F32(1.0) / jnp.sqrt(F32(total_rows))
    for m in range(3):
        flipped = jnp.transpose(terms[:, m * LANES : (m + 1) * LANES])
        forward[m * chan : (m + 1) * chan, :] = flipped[0:chan] * factor
    wgrad_ref[...] = forward[pl.ds(begin - tap0 * chan, shard), :][:, 0:chan]

    for delta in range(1, owners):
        reply_copy(delta).wait_send()
        reply_arrival(delta).wait_recv()
    answer = lax.dot_general(
        slot_mask(mine), returned[...].reshape(slot_n, 2 * LANES), (((0,), (0,)), ((), ())),
        preferred_element_type=F32,
    ).astype(BF16)
    out_ref[...] = answer[:, 0:chan]
    grad_ref[...] = answer[:, LANES : LANES + chan]


def window_shards(features, cotangent, keys, weight):
    rows, chan = features.shape
    wide_n, narrow_n, sub_n = (lax.axis_size(a) for a in ("wide", "narrow", "sub"))
    owners = wide_n * narrow_n
    cap = 2 * rows // owners
    half = DEPTH // sub_n
    cells = EDGE * EDGE * half
    shard = 27 * chan // (owners * sub_n)
    field = (EDGE * narrow_n + 2, DEPTH + 2, EDGE * wide_n + 2 * EDGE, LANES)
    near = (3, EDGE + 2, half + 2, EDGE, LANES)
    dims = (wide_n, narrow_n, sub_n, rows, chan, cap, shard)
    vmem = pl.BlockSpec(memory_space=pltpu.VMEM)
    out, grad, terms = pl.pallas_call(
        functools.partial(window_kernel, dims),
        out_shape=(
            jax.ShapeDtypeStruct((rows, chan), BF16),
            jax.ShapeDtypeStruct((rows, chan), BF16),
            jax.ShapeDtypeStruct((shard, chan), F32),
        ),
        in_specs=[vmem] * 4,
        out_specs=(vmem,) * 3,
        scratch_shapes=[
            pltpu.VMEM((owners * sub_n, rows + 16, 2 * LANES), BF16),
            pltpu.VMEM((sub_n, owners, owners, cap, 2 * LANES), BF16),
            pltpu.VMEM(field, F32),
            pltpu.VMEM(field, F32),
            pltpu.VMEM(near, BF16),
            pltpu.VMEM(near, BF16),
            pltpu.VMEM((27, LANES, LANES), BF16),
            pltpu.VMEM((cells, owners * cap), BF16),
            pltpu.VMEM((cells, LANES), F32),
            pltpu.VMEM((cells, LANES), F32),
            pltpu.VMEM((owners, cap, 2 * LANES), BF16),
            pltpu.VMEM((owners, cap, 2 * LANES), BF16),
            pltpu.VMEM((LANES, 3 * LANES), F32),
            pltpu.SemaphoreType.DMA((owners * sub_n, 4)),
            pltpu.SemaphoreType.DMA((owners * sub_n,)),
            pltpu.SemaphoreType.DMA((owners,)),
            pltpu.SemaphoreType.DMA((owners,)),
        ],
        compiler_params=pltpu.CompilerParams(
            collective_id=0, has_side_effects=True, vmem_limit_bytes=50 * 1024 * 1024
        ),
    )(features, cotangent, keys.reshape(1, rows), weight)
    return out, grad, terms.reshape(-1)


def extended(array, sides, width):
    for axis, dim in sides:
        size, length = (lax.axis_size(axis), array.shape[dim])
        up = [(i, (i + 1) % size) for i in range(size - 1)]
        down = [(j, i) for i, j in up]
        last = lax.slice_in_dim(array, length - width, length, axis=dim)
        first = lax.slice_in_dim(array, 0, width, axis=dim)
        before = lax.ppermute(last, axis, up)
        after = lax.ppermute(first, axis, down)
        array = jnp.concatenate([before, array, after], axis=dim)
    return array


def brick_pass(padded, weight, chan_count, half_depth):
    fields = padded[..., :chan_count]
    back_field = padded[..., chan_count:]
    centre = back_field[1:-1, 1:-1, 1:-1].reshape(-1, chan_count)
    cell_count = EDGE * EDGE * half_depth
    forward = jnp.zeros((cell_count, chan_count), jnp.float32)
    backward = jnp.zeros((cell_count, chan_count), jnp.float32)
    pieces = []
    for group in range(9):
        step_x = group // 3 - 1
        step_y = group % 3 - 1
        shifted = jnp.concatenate(
            [
                fields[
                    1 + step_x : 1 + step_x + EDGE,
                    1 + step_y : 1 + step_y + EDGE,
                    1 + step_z : 1 + step_z + half_depth,
                ]
                for step_z in (-1, 0, 1)
            ],
            axis=3,
        ).reshape(-1, 3 * chan_count)
        mirrored = jnp.concatenate(
            [
                back_field[
                    1 - step_x : 1 - step_x + EDGE,
                    1 - step_y : 1 - step_y + EDGE,
                    1 - step_z : 1 - step_z + half_depth,
                ]
                for step_z in (-1, 0, 1)
            ],
            axis=3,
        ).reshape(-1, 3 * chan_count)
        tap_block = weight[3 * group : 3 * group + 3]
        forward = forward + jnp.dot(
            shifted,
            tap_block.reshape(3 * chan_count, chan_count),
            preferred_element_type=jnp.float32,
        )
        backward = backward + jnp.dot(
            mirrored,
            jnp.transpose(tap_block, (0, 2, 1)).reshape(3 * chan_count, chan_count),
            preferred_element_type=jnp.float32,
        )
        pieces.append(
            lax.dot_general(
                shifted, centre, (((0,), (0,)), ((), ())), preferred_element_type=jnp.float32
            )
        )
    weight_terms = jnp.concatenate(pieces, axis=0)
    return (forward.astype(jnp.bfloat16), backward.astype(jnp.bfloat16), weight_terms)


def shards(features, cotangent, keys, weight):
    row_count, chan_count = features.shape
    wide_size = lax.axis_size("wide")
    narrow = lax.axis_size("narrow")
    sub_size = lax.axis_size("sub")
    owners = wide_size * narrow
    capacity = 2 * row_count // owners
    slot_count = owners * capacity
    half_depth = DEPTH // sub_size
    cell_count = EDGE * EDGE * half_depth
    target = keys // cell_count // sub_size
    local_cell = keys % cell_count
    columns = jnp.arange(owners, dtype=jnp.int32)
    before = jnp.sum((target[:, None] < columns[None, :]).astype(jnp.int32), axis=0)
    matches = target[:, None] == columns[None, :]
    first_row = jnp.sum(jnp.where(matches, before[None, :], 0), axis=1)
    row_rank = jnp.arange(row_count, dtype=jnp.int32) - first_row
    send_slot = target * capacity + row_rank
    payload = jnp.concatenate([features, cotangent], axis=1)
    outgoing = jnp.zeros((slot_count, 2 * chan_count), jnp.bfloat16).at[send_slot].set(payload)
    placed = jnp.full((slot_count,), -1, jnp.int32).at[send_slot].set(local_cell)
    incoming, arrived = (
        lax.all_to_all(outgoing, ("wide", "narrow"), split_axis=0, concat_axis=0, tiled=True),
        lax.all_to_all(placed, ("wide", "narrow"), split_axis=0, concat_axis=0, tiled=True),
    )
    is_live = arrived >= 0
    position = jnp.where(is_live, arrived, cell_count)
    dense = jnp.zeros((cell_count + 1, 2 * chan_count), jnp.bfloat16).at[position].set(incoming)
    dense = dense[:cell_count].reshape(EDGE, EDGE, half_depth, 2 * chan_count)
    padded = extended(dense, (("wide", 1), ("narrow", 0), ("sub", 2)), 1)
    outputs, gradient, weight_terms = brick_pass(padded, weight, chan_count, half_depth)
    reply = jnp.concatenate([outputs, gradient], axis=1)
    picked = jnp.where(
        is_live[:, None], reply[jnp.where(is_live, arrived, 0)], jnp.zeros((), jnp.bfloat16)
    )
    returned = lax.all_to_all(picked, ("wide", "narrow"), split_axis=0, concat_axis=0, tiled=True)
    answer = returned[send_slot]
    flat_terms = weight_terms.reshape(-1)
    partial_value = lax.psum_scatter(flat_terms, "wide", scatter_dimension=0, tiled=True)
    summed = lax.psum_scatter(partial_value, ("narrow", "sub"), scatter_dimension=0, tiled=True)
    factor = jnp.float32(1.0) / jnp.sqrt(jnp.float32(row_count * owners * sub_size))
    return (answer[:, :chan_count], answer[:, chan_count:], summed * factor)


def solution(mesh):
    placed = (
        P(("groups", "wide", "narrow", "sub"), None),
        P(("groups", "wide", "narrow", "sub"), None),
        P(("groups", "wide", "narrow", "sub")),
        P(),
    )
    sizes = mesh.shape
    gathered = sizes["wide"] * sizes["narrow"] <= 8 and sizes["narrow"] == 2 and sizes["sub"] == 2
    return jax.shard_map(
        window_shards if gathered else shards,
        mesh=mesh,
        in_specs=placed,
        out_specs=(
            P(("groups", "wide", "narrow", "sub"), None),
            P(("groups", "wide", "narrow", "sub"), None),
            P(("groups", "wide", "narrow", "sub")),
        ),
        check_vma=False,
    )
```

```python
import functools

import jax
import jax.numpy as jnp
from jax import lax
from jax.experimental import pallas as pl
from jax.experimental.pallas import tpu as pltpu
from jax.sharding import PartitionSpec as P

EDGE = 16
DEPTH = 4
LANES = 128
F32, BF16 = jnp.float32, jnp.bfloat16


def window_kernel(
    dims, feat_ref, cot_ref, keys_ref, weight_ref, out_ref, grad_ref, wgrad_ref,
    held, slots, x_field, g_field, x_near, g_near, taps, mask, forward, backward,
    picked, returned, terms, send_sem, recv_sem, reply_send, reply_recv,
):
    wide_n, narrow_n, sub_n, rows, chan, cap, shard = dims
    owners = wide_n * narrow_n
    slot_n = owners * cap
    half = DEPTH // sub_n
    cells = EDGE * EDGE * half
    w, n, s = lax.axis_index("wide"), lax.axis_index("narrow"), lax.axis_index("sub")
    me = w * narrow_n + n

    def number(wi, ni, si):
        return (wi * narrow_n + ni) * sub_n + si

    def place(wi, ni, si):
        return {"wide": wi, "narrow": ni, "sub": si}

    barrier = pltpu.get_barrier_semaphore()
    for delta in range(1, owners):
        peer = lax.rem(me + delta, owners)
        pl.semaphore_signal(
            barrier, inc=1, device_id=place(peer // narrow_n, peer % narrow_n, s),
            device_id_type=pl.DeviceIdType.MESH,
        )
    pl.semaphore_signal(
        barrier, inc=1, device_id=place(w, n, 1 - s), device_id_type=pl.DeviceIdType.MESH
    )

    keys = keys_ref[...]
    target = lax.shift_right_logical(keys, (cells * sub_n).bit_length() - 1)
    local = keys & (cells - 1)
    cell = (local >> 5) * 32 + (local & 1) * EDGE + ((local >> 1) & (EDGE - 1))
    first = jnp.zeros_like(keys)
    for o in range(1, owners):
        before = jnp.sum((target < o).astype(F32), axis=1, keepdims=True).astype(jnp.int32)
        first = jnp.where(target == o, before, first)
    slot = target * cap + lax.broadcasted_iota(jnp.int32, keys.shape, 1) - first
    cell1 = cell + 1
    line = lax.broadcasted_iota(jnp.int32, (LANES, rows), 0)
    digits = jnp.where(line == 0, slot >> 4, 0)
    digits = jnp.where(line == 1, slot & 15, digits)
    digits = jnp.where(line == chan, cell1 >> 4, digits)
    digits = jnp.where(line == chan + 1, cell1 & 15, digits)
    digits = digits.astype(F32).astype(BF16)
    eye = (
        lax.broadcasted_iota(jnp.int32, (rows, rows), 0)
        == lax.broadcasted_iota(jnp.int32, (rows, rows), 1)
    )
    eye = jnp.where(eye, 1.0, 0.0).astype(BF16)
    spare = jnp.zeros((LANES - chan, rows), BF16)
    lines_in = jnp.concatenate([feat_ref[...], digits[chan:LANES], cot_ref[...], spare], axis=0)
    packed = lax.dot_general(eye, lines_in, (((1,), (1,)), ((), ())), preferred_element_type=F32)
    mine = number(w, n, s)
    held[mine, 0:rows, :] = packed.astype(BF16)
    held[mine, rows : rows + 16, :] = digits[0:16]

    pl.semaphore_wait(barrier, owners)

    def block_copy(block, kind, target_place):
        return pltpu.make_async_remote_copy(
            src_ref=held.at[block], dst_ref=held.at[block],
            send_sem=send_sem.at[block, kind], recv_sem=recv_sem.at[block],
            device_id=target_place, device_id_type=pl.DeviceIdType.MESH,
        )

    up, down = place(w + 1, n, s), place(w - 1, n, s)
    across, sibling = place(w, 1 - n, s), place(w, n, 1 - s)

    @pl.when(w + 1 < wide_n)
    def _():
        block_copy(mine, 0, up).start()

    @pl.when(w >= 1)
    def _():
        block_copy(mine, 1, down).start()

    block_copy(mine, 2, across).start()
    block_copy(mine, 3, sibling).start()

    def clear(i, carry):
        x_field[i] = jnp.zeros(x_field.shape[1:], F32)
        g_field[i] = jnp.zeros(g_field.shape[1:], F32)
        return carry

    lax.fori_loop(0, x_field.shape[0], clear, 0)
    taps[...] = jnp.zeros(taps.shape, BF16)
    for t in range(27):
        taps[t, 0:chan, 0:chan] = weight_ref[t]

    def slot_mask(block):
        lines = held[block, rows : rows + 16, :].astype(F32)
        slot_of = lines[0:1] * 16.0 + lines[1:2]
        order = lax.broadcasted_iota(jnp.int32, (slot_n, rows), 0).astype(F32)
        return jnp.where(order == slot_of, 1.0, 0.0).astype(BF16)

    def to_slots(block):
        filled = jnp.dot(slot_mask(block), held[block, 0:rows, :], preferred_element_type=F32)
        source = block // sub_n
        slots[block % sub_n, :, source] = filled.astype(BF16).reshape(owners, cap, 2 * LANES)

    row_of = lax.broadcasted_iota(jnp.int32, (16, 2 * LANES), 0)
    lane_of = lax.broadcasted_iota(jnp.int32, (16, 2 * LANES), 1)
    chooser = jnp.where(lane_of == chan, 16.0, jnp.where(lane_of == chan + 1, 1.0, 0.0))
    chooser = jnp.where(row_of == 0, chooser, 0.0).astype(BF16)

    def cell_mask(block):
        rows_in = slots[block % sub_n, block // sub_n].reshape(slot_n, 2 * LANES)
        cell_of = lax.dot_general(
            chooser, rows_in, (((1,), (1,)), ((), ())), preferred_element_type=F32
        )[0:1]
        order = lax.broadcasted_iota(jnp.int32, (cells, slot_n), 0).astype(F32) + 1.0
        return jnp.where(order == cell_of, 1.0, 0.0).astype(BF16), rows_in

    def to_field(block):
        ones, rows_in = cell_mask(block)
        dense = jnp.dot(ones, rows_in, preferred_element_type=F32)
        dense = dense.reshape(EDGE, half, EDGE, 2 * LANES)
        owner = block // sub_n
        at = (
            pl.ds(1 + EDGE * (owner % narrow_n), EDGE),
            pl.ds(1 + half * (block % sub_n), half),
            pl.ds(pl.multiple_of(EDGE + EDGE * (owner // narrow_n), EDGE), EDGE),
        )
        x_field[at] = dense[..., 0:LANES]
        g_field[at] = dense[..., LANES : 2 * LANES]

    to_slots(mine)

    def offset(step):
        distance = (step + 1) // 2
        from_below = step % 2 == 1
        wi = jnp.where(from_below, w - distance, w + distance)
        return from_below, wi, jnp.logical_and(wi >= 0, wi < wide_n)

    def arrive(step, carry):
        from_below, wi, valid = offset(step)

        @pl.when(jnp.logical_and(valid, jnp.logical_and(step >= 1, step < 2 * wide_n - 1)))
        def _():
            block = number(wi, n, s)
            block_copy(block, 0, up).wait_recv()

            @pl.when(jnp.logical_and(from_below, w + 1 < wide_n))
            def _():
                block_copy(block, 0, up).start()

            @pl.when(jnp.logical_and(jnp.logical_not(from_below), w >= 1))
            def _():
                block_copy(block, 1, down).start()

            block_copy(block, 2, across).start()
            block_copy(block, 3, sibling).start()
            to_slots(block)

        _, wx, there = offset(step - 2)

        @pl.when(jnp.logical_and(there, step >= 2))
        def _():
            block = number(wx, 1 - n, s)
            block_copy(block, 2, across).wait_recv()
            block_copy(block, 3, sibling).start()
            to_slots(block)

        return carry

    lax.fori_loop(1, 2 * wide_n + 1, arrive, 0)

    def fields_of(si, begin, end):
        def one(i, carry):
            wi = lax.rem(w + wide_n - 1 + i // narrow_n, wide_n)
            to_field(number(wi, i % narrow_n, si))
            return carry

        lax.fori_loop(begin * narrow_n, end * narrow_n, one, 0)

    close = min(3, wide_n)
    fields_of(s, 0, close)

    def from_sibling(o, carry):
        block = o * sub_n + 1 - s
        block_copy(block, 3, sibling).wait_recv()
        to_slots(block)
        return carry

    lax.fori_loop(0, owners, from_sibling, 0)
    fields_of(1 - s, 0, close)
    mask[...] = cell_mask(mine)[0]

    wide_at = pl.ds(pl.multiple_of(EDGE * w, EDGE), 3 * EDGE)

    def near(i, carry):
        for k in range(half + 2):
            x_line = x_field[EDGE * n + i, half * s + k, wide_at, :]
            g_line = g_field[EDGE * n + i, half * s + k, wide_at, :]
            for j in range(3):
                begin = EDGE - 1 + j
                x_near[j, i, k] = x_line[begin : begin + EDGE].astype(BF16)
                g_near[j, i, k] = g_line[begin : begin + EDGE].astype(BF16)
        return carry

    lax.fori_loop(0, EDGE + 2, near, 0)

    forward[...] = jnp.zeros(forward.shape, F32)
    backward[...] = jnp.zeros(backward.shape, F32)

    def conv(group, carry):
        i, j = group // 3, group % 3
        ahead = jnp.concatenate(
            [x_near[j, pl.ds(i, EDGE), k : k + half].reshape(cells, LANES) for k in range(3)],
            axis=1,
        )
        behind = [
            g_near[2 - j, pl.ds(2 - i, EDGE), 2 - k : 2 - k + half].reshape(cells, LANES)
            for k in range(3)
        ]
        forward[...] += jnp.dot(
            ahead, taps[pl.ds(3 * group, 3)].reshape(3 * LANES, LANES), preferred_element_type=F32
        )
        total = backward[...]
        for k in range(3):
            total += lax.dot_general(
                behind[k], taps[3 * group + k], (((1,), (1,)), ((), ())),
                preferred_element_type=F32,
            )
        backward[...] = total
        return carry

    lax.fori_loop(0, 9, conv, 0)

    reply = jnp.concatenate([forward[...].astype(BF16), backward[...].astype(BF16)], axis=1)
    rows_out = lax.dot_general(
        mask[...], reply, (((0,), (0,)), ((), ())), preferred_element_type=F32
    ).astype(BF16)
    picked[...] = rows_out.reshape(owners, cap, 2 * LANES)

    def reply_copy(delta):
        peer = lax.rem(me + delta, owners)
        return pltpu.make_async_remote_copy(
            src_ref=picked.at[peer], dst_ref=returned.at[me],
            send_sem=reply_send.at[delta], recv_sem=reply_recv.at[delta],
            device_id=place(peer // narrow_n, peer % narrow_n, s),
            device_id_type=pl.DeviceIdType.MESH,
        )

    def reply_arrival(delta):
        peer = lax.rem(me + owners - delta, owners)
        return pltpu.make_async_remote_copy(
            src_ref=picked.at[peer], dst_ref=returned.at[peer],
            send_sem=reply_send.at[delta], recv_sem=reply_recv.at[delta],
            device_id=place(peer // narrow_n, peer % narrow_n, s),
            device_id_type=pl.DeviceIdType.MESH,
        )

    for delta in range(1, owners):
        reply_copy(delta).start()
    returned[me] = picked[me]

    fields_of(s, close, wide_n)
    fields_of(1 - s, close, wide_n)
    begin = mine * shard
    tap0 = begin // chan
    whole = EDGE * wide_n
    terms[...] = jnp.zeros(terms.shape, F32)
    steps = []
    for m in range(3):
        t = jnp.minimum(tap0 + m, 26)
        steps.append((t // 9, t // 3 % 3, t % 3))

    def gather(i, carry):
        right = []
        for a, b, c in steps:
            right.append(
                jnp.concatenate(
                    [
                        x_field[i + a, c + k, pl.ds(EDGE - 1 + b, whole), :].astype(BF16)
                        for k in range(DEPTH)
                    ],
                    axis=0,
                )
            )
        left = jnp.concatenate(
            [g_field[1 + i, 1 + k, EDGE : EDGE + whole, :].astype(BF16) for k in range(DEPTH)],
            axis=0,
        )
        terms[...] += lax.dot_general(
            left, jnp.concatenate(right, axis=1), (((0,), (0,)), ((), ())),
            preferred_element_type=F32,
        )
        return carry

    lax.fori_loop(0, EDGE * narrow_n, gather, 0)
    total_rows = rows * owners * sub_n
    factor = F32(1.0) / jnp.sqrt(F32(total_rows))
    for m in range(3):
        flipped = jnp.transpose(terms[:, m * LANES : (m + 1) * LANES])
        forward[m * chan : (m + 1) * chan, :] = flipped[0:chan] * factor
    wgrad_ref[...] = forward[pl.ds(begin - tap0 * chan, shard), :][:, 0:chan]

    for delta in range(1, owners):
        reply_copy(delta).wait_send()
        reply_arrival(delta).wait_recv()
    for wi in range(wide_n):
        block = number(wi, n, s)

        @pl.when(jnp.logical_and(wi <= w, w + 1 < wide_n))
        def _():
            block_copy(block, 0, up).wait_send()

        @pl.when(jnp.logical_and(wi >= w, w >= 1))
        def _():
            block_copy(block, 1, down).wait_send()

        block_copy(block, 2, across).wait_send()
        for ni in range(narrow_n):
            block_copy(number(wi, ni, s), 3, sibling).wait_send()

    answer = lax.dot_general(
        returned[...].reshape(slot_n, 2 * LANES), slot_mask(mine), (((0,), (0,)), ((), ())),
        preferred_element_type=F32,
    ).astype(BF16)
    out_ref[...] = answer[0:chan]
    grad_ref[...] = answer[LANES : LANES + chan]


def window_shards(features, cotangent, keys, weight):
    rows, chan = features.shape
    wide_n, narrow_n, sub_n = (lax.axis_size(a) for a in ("wide", "narrow", "sub"))
    owners = wide_n * narrow_n
    cap = 2 * rows // owners
    half = DEPTH // sub_n
    cells = EDGE * EDGE * half
    shard = 27 * chan // (owners * sub_n)
    field = (EDGE * narrow_n + 2, DEPTH + 2, EDGE * wide_n + 2 * EDGE, LANES)
    near = (3, EDGE + 2, half + 2, EDGE, LANES)
    dims = (wide_n, narrow_n, sub_n, rows, chan, cap, shard)
    vmem = pl.BlockSpec(memory_space=pltpu.VMEM)
    out, grad, terms = pl.pallas_call(
        functools.partial(window_kernel, dims),
        out_shape=(
            jax.ShapeDtypeStruct((chan, rows), BF16),
            jax.ShapeDtypeStruct((chan, rows), BF16),
            jax.ShapeDtypeStruct((shard, chan), F32),
        ),
        in_specs=[vmem] * 4,
        out_specs=(vmem,) * 3,
        scratch_shapes=[
            pltpu.VMEM((owners * sub_n, rows + 16, 2 * LANES), BF16),
            pltpu.VMEM((sub_n, owners, owners, cap, 2 * LANES), BF16),
            pltpu.VMEM(field, F32),
            pltpu.VMEM(field, F32),
            pltpu.VMEM(near, BF16),
            pltpu.VMEM(near, BF16),
            pltpu.VMEM((27, LANES, LANES), BF16),
            pltpu.VMEM((cells, owners * cap), BF16),
            pltpu.VMEM((cells, LANES), F32),
            pltpu.VMEM((cells, LANES), F32),
            pltpu.VMEM((owners, cap, 2 * LANES), BF16),
            pltpu.VMEM((owners, cap, 2 * LANES), BF16),
            pltpu.VMEM((LANES, 3 * LANES), F32),
            pltpu.SemaphoreType.DMA((owners * sub_n, 4)),
            pltpu.SemaphoreType.DMA((owners * sub_n,)),
            pltpu.SemaphoreType.DMA((owners,)),
            pltpu.SemaphoreType.DMA((owners,)),
        ],
        compiler_params=pltpu.CompilerParams(
            collective_id=0, has_side_effects=True, vmem_limit_bytes=50 * 1024 * 1024
        ),
    )(features.T, cotangent.T, keys.reshape(1, rows), weight)
    return out.T, grad.T, terms.reshape(-1)


def extended(array, sides, width):
    for axis, dim in sides:
        size, length = (lax.axis_size(axis), array.shape[dim])
        up = [(i, (i + 1) % size) for i in range(size - 1)]
        down = [(j, i) for i, j in up]
        last = lax.slice_in_dim(array, length - width, length, axis=dim)
        first = lax.slice_in_dim(array, 0, width, axis=dim)
        before = lax.ppermute(last, axis, up)
        after = lax.ppermute(first, axis, down)
        array = jnp.concatenate([before, array, after], axis=dim)
    return array


def brick_pass(padded, weight, chan_count, half_depth):
    fields = padded[..., :chan_count]
    back_field = padded[..., chan_count:]
    centre = back_field[1:-1, 1:-1, 1:-1].reshape(-1, chan_count)
    cell_count = EDGE * EDGE * half_depth
    forward = jnp.zeros((cell_count, chan_count), jnp.float32)
    backward = jnp.zeros((cell_count, chan_count), jnp.float32)
    pieces = []
    for group in range(9):
        step_x = group // 3 - 1
        step_y = group % 3 - 1
        shifted = jnp.concatenate(
            [
                fields[
                    1 + step_x : 1 + step_x + EDGE,
                    1 + step_y : 1 + step_y + EDGE,
                    1 + step_z : 1 + step_z + half_depth,
                ]
                for step_z in (-1, 0, 1)
            ],
            axis=3,
        ).reshape(-1, 3 * chan_count)
        mirrored = jnp.concatenate(
            [
                back_field[
                    1 - step_x : 1 - step_x + EDGE,
                    1 - step_y : 1 - step_y + EDGE,
                    1 - step_z : 1 - step_z + half_depth,
                ]
                for step_z in (-1, 0, 1)
            ],
            axis=3,
        ).reshape(-1, 3 * chan_count)
        tap_block = weight[3 * group : 3 * group + 3]
        forward = forward + jnp.dot(
            shifted,
            tap_block.reshape(3 * chan_count, chan_count),
            preferred_element_type=jnp.float32,
        )
        backward = backward + jnp.dot(
            mirrored,
            jnp.transpose(tap_block, (0, 2, 1)).reshape(3 * chan_count, chan_count),
            preferred_element_type=jnp.float32,
        )
        pieces.append(
            lax.dot_general(
                shifted, centre, (((0,), (0,)), ((), ())), preferred_element_type=jnp.float32
            )
        )
    weight_terms = jnp.concatenate(pieces, axis=0)
    return (forward.astype(jnp.bfloat16), backward.astype(jnp.bfloat16), weight_terms)


def shards(features, cotangent, keys, weight):
    row_count, chan_count = features.shape
    wide_size = lax.axis_size("wide")
    narrow = lax.axis_size("narrow")
    sub_size = lax.axis_size("sub")
    owners = wide_size * narrow
    capacity = 2 * row_count // owners
    slot_count = owners * capacity
    half_depth = DEPTH // sub_size
    cell_count = EDGE * EDGE * half_depth
    target = keys // cell_count // sub_size
    local_cell = keys % cell_count
    columns = jnp.arange(owners, dtype=jnp.int32)
    before = jnp.sum((target[:, None] < columns[None, :]).astype(jnp.int32), axis=0)
    matches = target[:, None] == columns[None, :]
    first_row = jnp.sum(jnp.where(matches, before[None, :], 0), axis=1)
    row_rank = jnp.arange(row_count, dtype=jnp.int32) - first_row
    send_slot = target * capacity + row_rank
    payload = jnp.concatenate([features, cotangent], axis=1)
    outgoing = jnp.zeros((slot_count, 2 * chan_count), jnp.bfloat16).at[send_slot].set(payload)
    placed = jnp.full((slot_count,), -1, jnp.int32).at[send_slot].set(local_cell)
    incoming, arrived = (
        lax.all_to_all(outgoing, ("wide", "narrow"), split_axis=0, concat_axis=0, tiled=True),
        lax.all_to_all(placed, ("wide", "narrow"), split_axis=0, concat_axis=0, tiled=True),
    )
    is_live = arrived >= 0
    position = jnp.where(is_live, arrived, cell_count)
    dense = jnp.zeros((cell_count + 1, 2 * chan_count), jnp.bfloat16).at[position].set(incoming)
    dense = dense[:cell_count].reshape(EDGE, EDGE, half_depth, 2 * chan_count)
    padded = extended(dense, (("wide", 1), ("narrow", 0), ("sub", 2)), 1)
    outputs, gradient, weight_terms = brick_pass(padded, weight, chan_count, half_depth)
    reply = jnp.concatenate([outputs, gradient], axis=1)
    picked = jnp.where(
        is_live[:, None], reply[jnp.where(is_live, arrived, 0)], jnp.zeros((), jnp.bfloat16)
    )
    returned = lax.all_to_all(picked, ("wide", "narrow"), split_axis=0, concat_axis=0, tiled=True)
    answer = returned[send_slot]
    flat_terms = weight_terms.reshape(-1)
    partial_value = lax.psum_scatter(flat_terms, "wide", scatter_dimension=0, tiled=True)
    summed = lax.psum_scatter(partial_value, ("narrow", "sub"), scatter_dimension=0, tiled=True)
    factor = jnp.float32(1.0) / jnp.sqrt(jnp.float32(row_count * owners * sub_size))
    return (answer[:, :chan_count], answer[:, chan_count:], summed * factor)


def solution(mesh):
    placed = (
        P(("groups", "wide", "narrow", "sub"), None),
        P(("groups", "wide", "narrow", "sub"), None),
        P(("groups", "wide", "narrow", "sub")),
        P(),
    )
    sizes = mesh.shape
    gathered = sizes["wide"] * sizes["narrow"] <= 8 and sizes["narrow"] == 2 and sizes["sub"] == 2
    return jax.shard_map(
        window_shards if gathered else shards,
        mesh=mesh,
        in_specs=placed,
        out_specs=(
            P(("groups", "wide", "narrow", "sub"), None),
            P(("groups", "wide", "narrow", "sub"), None),
            P(("groups", "wide", "narrow", "sub")),
        ),
        check_vma=False,
    )
```

```python
import functools

import jax
import jax.numpy as jnp
from jax import lax
from jax.experimental import pallas as pl
from jax.experimental.pallas import tpu as pltpu
from jax.sharding import PartitionSpec as P

EDGE = 16
DEPTH = 4
LANES = 128
F32, BF16 = jnp.float32, jnp.bfloat16


def window_kernel(
    dims, feat_in, cot_in, keys_in, weight_in, out_ref, grad_ref, wgrad_ref,
    held, slots, x_field, g_field, x_near, g_near, taps, mask, forward, backward,
    picked, returned, terms, feat_ref, cot_ref, keys_ref, weight_ref, cell_rows, fetch_sem, send_sem, recv_sem, reply_send, reply_recv,
):
    wide_n, narrow_n, sub_n, rows, chan, cap, shard = dims
    owners = wide_n * narrow_n
    slot_n = owners * cap
    half = DEPTH // sub_n
    cells = EDGE * EDGE * half
    w, n, s = lax.axis_index("wide"), lax.axis_index("narrow"), lax.axis_index("sub")
    me = w * narrow_n + n

    def number(wi, ni, si):
        return (wi * narrow_n + ni) * sub_n + si

    def place(wi, ni, si):
        return {"wide": wi, "narrow": ni, "sub": si}

    fetches = [
        pltpu.make_async_copy(source, goal, fetch_sem.at[i])
        for i, (source, goal) in enumerate(
            ((keys_in, keys_ref), (feat_in, feat_ref), (cot_in, cot_ref), (weight_in, weight_ref))
        )
    ]
    for fetch in fetches:
        fetch.start()

    barrier = pltpu.get_barrier_semaphore()
    for delta in range(1, owners):
        peer = lax.rem(me + delta, owners)
        pl.semaphore_signal(
            barrier, inc=1, device_id=place(peer // narrow_n, peer % narrow_n, s),
            device_id_type=pl.DeviceIdType.MESH,
        )
    pl.semaphore_signal(
        barrier, inc=1, device_id=place(w, n, 1 - s), device_id_type=pl.DeviceIdType.MESH
    )

    fetches[0].wait()
    keys = keys_ref[...]
    target = lax.shift_right_logical(keys, (cells * sub_n).bit_length() - 1)
    local = keys & (cells - 1)
    cell = (local >> 5) * 32 + (local & 1) * EDGE + ((local >> 1) & (EDGE - 1))
    first = jnp.zeros_like(keys)
    for o in range(1, owners):
        before = jnp.sum((target < o).astype(F32), axis=1, keepdims=True).astype(jnp.int32)
        first = jnp.where(target == o, before, first)
    slot = target * cap + lax.broadcasted_iota(jnp.int32, keys.shape, 1) - first
    cell1 = cell + 1
    line = lax.broadcasted_iota(jnp.int32, (LANES, rows), 0)
    digits = jnp.where(line == 0, slot >> 4, 0)
    digits = jnp.where(line == 1, slot & 15, digits)
    digits = jnp.where(line == chan, cell1 >> 4, digits)
    digits = jnp.where(line == chan + 1, cell1 & 15, digits)
    digits = digits.astype(F32).astype(BF16)
    eye = (
        lax.broadcasted_iota(jnp.int32, (rows, rows), 0)
        == lax.broadcasted_iota(jnp.int32, (rows, rows), 1)
    )
    eye = jnp.where(eye, 1.0, 0.0).astype(BF16)
    fetches[1].wait()
    fetches[2].wait()
    spare = jnp.zeros((LANES - chan, rows), BF16)
    lines_in = jnp.concatenate([feat_ref[...], digits[chan:LANES], cot_ref[...], spare], axis=0)
    packed = lax.dot_general(eye, lines_in, (((1,), (1,)), ((), ())), preferred_element_type=F32)
    mine = number(w, n, s)
    held[mine, 0:rows, :] = packed.astype(BF16)
    held[mine, rows : rows + 16, :] = digits[0:16]

    pl.semaphore_wait(barrier, owners)

    def block_copy(block, kind, target_place):
        return pltpu.make_async_remote_copy(
            src_ref=held.at[block], dst_ref=held.at[block],
            send_sem=send_sem.at[block, kind], recv_sem=recv_sem.at[block],
            device_id=target_place, device_id_type=pl.DeviceIdType.MESH,
        )

    across, sibling = place(w, 1 - n, s), place(w, n, 1 - s)
    last, inner = wide_n - 1, wide_n

    def along(distance, above):
        peer = w + distance if above else w - distance
        kind = lax.rem(peer - w + wide_n, wide_n) - 1
        return block_copy(mine, kind, place(peer, n, s))

    block_copy(mine, last, across).start()
    for distance in range(1, wide_n):

        @pl.when(w + distance < wide_n)
        def _():
            along(distance, True).start()

        @pl.when(w >= distance)
        def _():
            along(distance, False).start()

    block_copy(mine, inner, sibling).start()

    def clear(i, carry):
        x_field[i] = jnp.zeros(x_field.shape[1:], F32)
        g_field[i] = jnp.zeros(g_field.shape[1:], F32)
        return carry

    lax.fori_loop(0, x_field.shape[0], clear, 0)
    taps[...] = jnp.zeros(taps.shape, BF16)
    fetches[3].wait()
    for t in range(27):
        taps[t, 0:chan, 0:chan] = weight_ref[t]

    def slot_mask(block):
        lines = held[block, rows : rows + 16, :].astype(F32)
        slot_of = lines[0:1] * 16.0 + lines[1:2]
        order = lax.broadcasted_iota(jnp.int32, (slot_n, rows), 0).astype(F32)
        return jnp.where(order == slot_of, 1.0, 0.0).astype(BF16)

    def to_slots(block):
        filled = jnp.dot(slot_mask(block), held[block, 0:rows, :], preferred_element_type=F32)
        source = block // sub_n
        slots[block % sub_n, :, source] = filled.astype(BF16).reshape(owners, cap, 2 * LANES)

    row_of = lax.broadcasted_iota(jnp.int32, (16, 2 * LANES), 0)
    lane_of = lax.broadcasted_iota(jnp.int32, (16, 2 * LANES), 1)
    chooser = jnp.where(lane_of == chan, 16.0, jnp.where(lane_of == chan + 1, 1.0, 0.0))
    chooser = jnp.where(row_of == 0, chooser, 0.0).astype(BF16)

    def find_cells(si):
        found = lax.dot_general(
            chooser, slots[si].reshape(owners * slot_n, 2 * LANES), (((1,), (1,)), ((), ())),
            preferred_element_type=F32,
        )
        for o in range(owners):
            cell_rows[si, o] = found[0:8, o * slot_n : (o + 1) * slot_n]

    def cell_mask(block):
        cell_of = cell_rows[block % sub_n, block // sub_n][0:1]
        order = lax.broadcasted_iota(jnp.int32, (cells, slot_n), 0).astype(F32) + 1.0
        return jnp.where(order == cell_of, 1.0, 0.0).astype(BF16)

    def to_field(block):
        rows_in = slots[block % sub_n, block // sub_n].reshape(slot_n, 2 * LANES)
        dense = jnp.dot(cell_mask(block), rows_in, preferred_element_type=F32)
        dense = dense.reshape(EDGE, half, EDGE, 2 * LANES)
        owner = block // sub_n
        at = (
            pl.ds(1 + EDGE * (owner % narrow_n), EDGE),
            pl.ds(1 + half * (block % sub_n), half),
            pl.ds(pl.multiple_of(EDGE + EDGE * (owner // narrow_n), EDGE), EDGE),
        )
        x_field[at] = dense[..., 0:LANES]
        g_field[at] = dense[..., LANES : 2 * LANES]

    to_slots(mine)

    def offset(step):
        distance = (step + 1) // 2
        wi = jnp.where(step % 2 == 1, w - distance, w + distance)
        return wi, jnp.logical_and(wi >= 0, wi < wide_n)

    def arrive(step, carry):
        wi, valid = offset(step)

        @pl.when(jnp.logical_and(valid, jnp.logical_and(step >= 1, step < 2 * wide_n - 1)))
        def _():
            block = number(wi, n, s)
            block_copy(block, last, across).wait_recv()
            block_copy(block, last, across).start()
            block_copy(block, inner, sibling).start()
            to_slots(block)

        wx, there = offset(step - 2)

        @pl.when(jnp.logical_and(there, step >= 2))
        def _():
            block = number(wx, 1 - n, s)
            block_copy(block, last, across).wait_recv()
            block_copy(block, inner, sibling).start()
            to_slots(block)

        return carry

    lax.fori_loop(1, 2 * wide_n + 1, arrive, 0)

    def fields_of(si, begin, end):
        def one(i, carry):
            wi = lax.rem(w + wide_n - 1 + i // narrow_n, wide_n)
            to_field(number(wi, i % narrow_n, si))
            return carry

        lax.fori_loop(begin * narrow_n, end * narrow_n, one, 0, unroll=2)

    close = min(3, wide_n)
    find_cells(s)
    fields_of(s, 0, close)

    def from_sibling(o, carry):
        block = o * sub_n + 1 - s
        block_copy(block, inner, sibling).wait_recv()
        to_slots(block)
        return carry

    lax.fori_loop(0, owners, from_sibling, 0)
    find_cells(1 - s)
    fields_of(1 - s, 0, close)
    mask[...] = cell_mask(mine)

    wide_at = pl.ds(pl.multiple_of(EDGE * w, EDGE), 3 * EDGE)

    def near(i, carry):
        for k in range(half + 2):
            x_line = x_field[EDGE * n + i, half * s + k, wide_at, :]
            g_line = g_field[EDGE * n + i, half * s + k, wide_at, :]
            for j in range(3):
                begin = EDGE - 1 + j
                x_near[j, i, k] = x_line[begin : begin + EDGE].astype(BF16)
                g_near[j, i, k] = g_line[begin : begin + EDGE].astype(BF16)
        return carry

    lax.fori_loop(0, EDGE + 2, near, 0)

    forward[...] = jnp.zeros(forward.shape, F32)
    backward[...] = jnp.zeros(backward.shape, F32)

    def conv(group, carry):
        i, j = group // 3, group % 3
        ahead = jnp.concatenate(
            [x_near[j, pl.ds(i, EDGE), k : k + half].reshape(cells, LANES) for k in range(3)],
            axis=1,
        )
        behind = [
            g_near[2 - j, pl.ds(2 - i, EDGE), 2 - k : 2 - k + half].reshape(cells, LANES)
            for k in range(3)
        ]
        forward[...] += jnp.dot(
            ahead, taps[pl.ds(3 * group, 3)].reshape(3 * LANES, LANES), preferred_element_type=F32
        )
        total = backward[...]
        for k in range(3):
            total += lax.dot_general(
                behind[k], taps[3 * group + k], (((1,), (1,)), ((), ())),
                preferred_element_type=F32,
            )
        backward[...] = total
        return carry

    lax.fori_loop(0, 9, conv, 0)

    reply = jnp.concatenate([forward[...].astype(BF16), backward[...].astype(BF16)], axis=1)
    rows_out = lax.dot_general(
        mask[...], reply, (((0,), (0,)), ((), ())), preferred_element_type=F32
    ).astype(BF16)
    picked[...] = rows_out.reshape(owners, cap, 2 * LANES)

    def reply_copy(delta):
        peer = lax.rem(me + delta, owners)
        return pltpu.make_async_remote_copy(
            src_ref=picked.at[peer], dst_ref=returned.at[me],
            send_sem=reply_send.at[delta], recv_sem=reply_recv.at[delta],
            device_id=place(peer // narrow_n, peer % narrow_n, s),
            device_id_type=pl.DeviceIdType.MESH,
        )

    def reply_arrival(delta):
        peer = lax.rem(me + owners - delta, owners)
        return pltpu.make_async_remote_copy(
            src_ref=picked.at[peer], dst_ref=returned.at[peer],
            send_sem=reply_send.at[delta], recv_sem=reply_recv.at[delta],
            device_id=place(peer // narrow_n, peer % narrow_n, s),
            device_id_type=pl.DeviceIdType.MESH,
        )

    for delta in range(1, owners):
        reply_copy(delta).start()
    returned[me] = picked[me]

    fields_of(s, close, wide_n)
    fields_of(1 - s, close, wide_n)
    begin = mine * shard
    tap0 = begin // chan
    whole = EDGE * wide_n
    terms[...] = jnp.zeros(terms.shape, F32)
    steps = []
    for m in range(3):
        t = jnp.minimum(tap0 + m, 26)
        steps.append((t // 9, t // 3 % 3, t % 3))

    def gather(i, carry):
        right = []
        for a, b, c in steps:
            right.append(
                jnp.concatenate(
                    [
                        x_field[i + a, c + k, pl.ds(EDGE - 1 + b, whole), :].astype(BF16)
                        for k in range(DEPTH)
                    ],
                    axis=0,
                )
            )
        left = jnp.concatenate(
            [g_field[1 + i, 1 + k, EDGE : EDGE + whole, :].astype(BF16) for k in range(DEPTH)],
            axis=0,
        )
        terms[...] += lax.dot_general(
            left, jnp.concatenate(right, axis=1), (((0,), (0,)), ((), ())),
            preferred_element_type=F32,
        )
        return carry

    lax.fori_loop(0, EDGE * narrow_n, gather, 0)
    total_rows = rows * owners * sub_n
    factor = F32(1.0) / jnp.sqrt(F32(total_rows))
    for m in range(3):
        flipped = jnp.transpose(terms[:, m * LANES : (m + 1) * LANES])
        forward[m * chan : (m + 1) * chan, :] = flipped[0:chan] * factor
    wgrad_ref[...] = forward[pl.ds(begin - tap0 * chan, shard), :][:, 0:chan]

    for delta in range(1, owners):
        reply_copy(delta).wait_send()
        reply_arrival(delta).wait_recv()
    for delta in range(1, wide_n):
        block_copy(mine, delta - 1, across).wait_send()
    for wi in range(wide_n):
        block = number(wi, n, s)
        block_copy(block, last, across).wait_send()
        for ni in range(narrow_n):
            block_copy(number(wi, ni, s), inner, sibling).wait_send()

    answer = lax.dot_general(
        returned[...].reshape(slot_n, 2 * LANES), slot_mask(mine), (((0,), (0,)), ((), ())),
        preferred_element_type=F32,
    ).astype(BF16)
    out_ref[...] = answer[0:chan]
    grad_ref[...] = answer[LANES : LANES + chan]


def window_shards(features, cotangent, keys, weight):
    rows, chan = features.shape
    wide_n, narrow_n, sub_n = (lax.axis_size(a) for a in ("wide", "narrow", "sub"))
    owners = wide_n * narrow_n
    cap = 2 * rows // owners
    half = DEPTH // sub_n
    cells = EDGE * EDGE * half
    shard = 27 * chan // (owners * sub_n)
    field = (EDGE * narrow_n + 2, DEPTH + 2, EDGE * wide_n + 2 * EDGE, LANES)
    near = (3, EDGE + 2, half + 2, EDGE, LANES)
    dims = (wide_n, narrow_n, sub_n, rows, chan, cap, shard)
    vmem = pl.BlockSpec(memory_space=pltpu.VMEM)
    out, grad, terms = pl.pallas_call(
        functools.partial(window_kernel, dims),
        out_shape=(
            jax.ShapeDtypeStruct((chan, rows), BF16),
            jax.ShapeDtypeStruct((chan, rows), BF16),
            jax.ShapeDtypeStruct((shard, chan), F32),
        ),
        in_specs=[pl.BlockSpec(memory_space=pltpu.HBM)] * 4,
        out_specs=(vmem,) * 3,
        scratch_shapes=[
            pltpu.VMEM((owners * sub_n, rows + 16, 2 * LANES), BF16),
            pltpu.VMEM((sub_n, owners, owners, cap, 2 * LANES), BF16),
            pltpu.VMEM(field, F32),
            pltpu.VMEM(field, F32),
            pltpu.VMEM(near, BF16),
            pltpu.VMEM(near, BF16),
            pltpu.VMEM((27, LANES, LANES), BF16),
            pltpu.VMEM((cells, owners * cap), BF16),
            pltpu.VMEM((cells, LANES), F32),
            pltpu.VMEM((cells, LANES), F32),
            pltpu.VMEM((owners, cap, 2 * LANES), BF16),
            pltpu.VMEM((owners, cap, 2 * LANES), BF16),
            pltpu.VMEM((LANES, 3 * LANES), F32),
            pltpu.VMEM((chan, rows), BF16),
            pltpu.VMEM((chan, rows), BF16),
            pltpu.VMEM((1, rows), jnp.int32),
            pltpu.VMEM((27, chan, chan), BF16),
            pltpu.VMEM((sub_n, owners, 8, owners * cap), F32),
            pltpu.SemaphoreType.DMA((4,)),
            pltpu.SemaphoreType.DMA((owners * sub_n, wide_n + 1)),
            pltpu.SemaphoreType.DMA((owners * sub_n,)),
            pltpu.SemaphoreType.DMA((owners,)),
            pltpu.SemaphoreType.DMA((owners,)),
        ],
        compiler_params=pltpu.CompilerParams(
            collective_id=0, has_side_effects=True, vmem_limit_bytes=63 * 1024 * 1024
        ),
    )(features.T, cotangent.T, keys.reshape(1, rows), weight)
    return out.T, grad.T, terms.reshape(-1)


def extended(array, sides, width):
    for axis, dim in sides:
        size, length = (lax.axis_size(axis), array.shape[dim])
        up = [(i, (i + 1) % size) for i in range(size - 1)]
        down = [(j, i) for i, j in up]
        last = lax.slice_in_dim(array, length - width, length, axis=dim)
        first = lax.slice_in_dim(array, 0, width, axis=dim)
        before = lax.ppermute(last, axis, up)
        after = lax.ppermute(first, axis, down)
        array = jnp.concatenate([before, array, after], axis=dim)
    return array


def brick_pass(padded, weight, chan_count, half_depth):
    fields = padded[..., :chan_count]
    back_field = padded[..., chan_count:]
    centre = back_field[1:-1, 1:-1, 1:-1].reshape(-1, chan_count)
    cell_count = EDGE * EDGE * half_depth
    forward = jnp.zeros((cell_count, chan_count), jnp.float32)
    backward = jnp.zeros((cell_count, chan_count), jnp.float32)
    pieces = []
    for group in range(9):
        step_x = group // 3 - 1
        step_y = group % 3 - 1
        shifted = jnp.concatenate(
            [
                fields[
                    1 + step_x : 1 + step_x + EDGE,
                    1 + step_y : 1 + step_y + EDGE,
                    1 + step_z : 1 + step_z + half_depth,
                ]
                for step_z in (-1, 0, 1)
            ],
            axis=3,
        ).reshape(-1, 3 * chan_count)
        mirrored = jnp.concatenate(
            [
                back_field[
                    1 - step_x : 1 - step_x + EDGE,
                    1 - step_y : 1 - step_y + EDGE,
                    1 - step_z : 1 - step_z + half_depth,
                ]
                for step_z in (-1, 0, 1)
            ],
            axis=3,
        ).reshape(-1, 3 * chan_count)
        tap_block = weight[3 * group : 3 * group + 3]
        forward = forward + jnp.dot(
            shifted,
            tap_block.reshape(3 * chan_count, chan_count),
            preferred_element_type=jnp.float32,
        )
        backward = backward + jnp.dot(
            mirrored,
            jnp.transpose(tap_block, (0, 2, 1)).reshape(3 * chan_count, chan_count),
            preferred_element_type=jnp.float32,
        )
        pieces.append(
            lax.dot_general(
                shifted, centre, (((0,), (0,)), ((), ())), preferred_element_type=jnp.float32
            )
        )
    weight_terms = jnp.concatenate(pieces, axis=0)
    return (forward.astype(jnp.bfloat16), backward.astype(jnp.bfloat16), weight_terms)


def shards(features, cotangent, keys, weight):
    row_count, chan_count = features.shape
    wide_size = lax.axis_size("wide")
    narrow = lax.axis_size("narrow")
    sub_size = lax.axis_size("sub")
    owners = wide_size * narrow
    capacity = 2 * row_count // owners
    slot_count = owners * capacity
    half_depth = DEPTH // sub_size
    cell_count = EDGE * EDGE * half_depth
    target = keys // cell_count // sub_size
    local_cell = keys % cell_count
    columns = jnp.arange(owners, dtype=jnp.int32)
    before = jnp.sum((target[:, None] < columns[None, :]).astype(jnp.int32), axis=0)
    matches = target[:, None] == columns[None, :]
    first_row = jnp.sum(jnp.where(matches, before[None, :], 0), axis=1)
    row_rank = jnp.arange(row_count, dtype=jnp.int32) - first_row
    send_slot = target * capacity + row_rank
    payload = jnp.concatenate([features, cotangent], axis=1)
    outgoing = jnp.zeros((slot_count, 2 * chan_count), jnp.bfloat16).at[send_slot].set(payload)
    placed = jnp.full((slot_count,), -1, jnp.int32).at[send_slot].set(local_cell)
    incoming, arrived = (
        lax.all_to_all(outgoing, ("wide", "narrow"), split_axis=0, concat_axis=0, tiled=True),
        lax.all_to_all(placed, ("wide", "narrow"), split_axis=0, concat_axis=0, tiled=True),
    )
    is_live = arrived >= 0
    position = jnp.where(is_live, arrived, cell_count)
    dense = jnp.zeros((cell_count + 1, 2 * chan_count), jnp.bfloat16).at[position].set(incoming)
    dense = dense[:cell_count].reshape(EDGE, EDGE, half_depth, 2 * chan_count)
    padded = extended(dense, (("wide", 1), ("narrow", 0), ("sub", 2)), 1)
    outputs, gradient, weight_terms = brick_pass(padded, weight, chan_count, half_depth)
    reply = jnp.concatenate([outputs, gradient], axis=1)
    picked = jnp.where(
        is_live[:, None], reply[jnp.where(is_live, arrived, 0)], jnp.zeros((), jnp.bfloat16)
    )
    returned = lax.all_to_all(picked, ("wide", "narrow"), split_axis=0, concat_axis=0, tiled=True)
    answer = returned[send_slot]
    flat_terms = weight_terms.reshape(-1)
    partial_value = lax.psum_scatter(flat_terms, "wide", scatter_dimension=0, tiled=True)
    summed = lax.psum_scatter(partial_value, ("narrow", "sub"), scatter_dimension=0, tiled=True)
    factor = jnp.float32(1.0) / jnp.sqrt(jnp.float32(row_count * owners * sub_size))
    return (answer[:, :chan_count], answer[:, chan_count:], summed * factor)


def solution(mesh):
    placed = (
        P(("groups", "wide", "narrow", "sub"), None),
        P(("groups", "wide", "narrow", "sub"), None),
        P(("groups", "wide", "narrow", "sub")),
        P(),
    )
    sizes = mesh.shape
    gathered = sizes["wide"] * sizes["narrow"] <= 8 and sizes["narrow"] == 2 and sizes["sub"] == 2
    return jax.shard_map(
        window_shards if gathered else shards,
        mesh=mesh,
        in_specs=placed,
        out_specs=(
            P(("groups", "wide", "narrow", "sub"), None),
            P(("groups", "wide", "narrow", "sub"), None),
            P(("groups", "wide", "narrow", "sub")),
        ),
        check_vma=False,
    )
```

```python
import functools

import jax
import jax.numpy as jnp
from jax import lax
from jax.experimental import pallas as pl
from jax.experimental.pallas import tpu as pltpu
from jax.sharding import PartitionSpec as P

EDGE = 16
DEPTH = 4
LANES = 128
F32, BF16 = jnp.float32, jnp.bfloat16


def window_kernel(
    dims, feat_in, cot_in, keys_in, weight_in, out_ref, grad_ref, wgrad_ref,
    held, slots, x_field, g_field, x_near, g_near, taps, mask, forward, backward,
    picked, returned, terms, feat_ref, cot_ref, keys_ref, weight_ref, cell_rows, fetch_sem, send_sem, recv_sem, reply_send, reply_recv,
):
    wide_n, narrow_n, sub_n, rows, chan, cap, shard = dims
    owners = wide_n * narrow_n
    slot_n = owners * cap
    half = DEPTH // sub_n
    cells = EDGE * EDGE * half
    w, n, s = lax.axis_index("wide"), lax.axis_index("narrow"), lax.axis_index("sub")
    me = w * narrow_n + n

    def number(wi, ni, si):
        return (wi * narrow_n + ni) * sub_n + si

    def place(wi, ni, si):
        return {"wide": wi, "narrow": ni, "sub": si}

    fetches = [
        pltpu.make_async_copy(source, goal, fetch_sem.at[i])
        for i, (source, goal) in enumerate(
            ((keys_in, keys_ref), (feat_in, feat_ref), (cot_in, cot_ref), (weight_in, weight_ref))
        )
    ]
    for fetch in fetches:
        fetch.start()

    barrier = pltpu.get_barrier_semaphore()
    for delta in range(1, owners):
        peer = lax.rem(me + delta, owners)
        pl.semaphore_signal(
            barrier, inc=1, device_id=place(peer // narrow_n, peer % narrow_n, s),
            device_id_type=pl.DeviceIdType.MESH,
        )
    pl.semaphore_signal(
        barrier, inc=1, device_id=place(w, n, 1 - s), device_id_type=pl.DeviceIdType.MESH
    )

    fetches[0].wait()
    keys = keys_ref[...]
    target = lax.shift_right_logical(keys, (cells * sub_n).bit_length() - 1)
    local = keys & (cells - 1)
    cell = (local >> 5) * 32 + (local & 1) * EDGE + ((local >> 1) & (EDGE - 1))
    first = jnp.zeros_like(keys)
    for o in range(1, owners):
        before = jnp.sum((target < o).astype(F32), axis=1, keepdims=True).astype(jnp.int32)
        first = jnp.where(target == o, before, first)
    slot = target * cap + lax.broadcasted_iota(jnp.int32, keys.shape, 1) - first
    cell1 = cell + 1
    line = lax.broadcasted_iota(jnp.int32, (16, rows), 0)
    digits = jnp.where(line == 0, slot >> 4, 0)
    digits = jnp.where(line == 1, slot & 15, digits)
    digits = jnp.where(line == 2, cell1 >> 4, digits)
    digits = jnp.where(line == 3, cell1 & 15, digits)
    digits = digits.astype(F32).astype(BF16)
    fetches[1].wait()
    fetches[2].wait()
    mine = number(w, n, s)
    held[mine, 0:chan, :] = feat_ref[...]
    held[mine, chan : chan + 16, :] = digits
    held[mine, chan + 16 : 2 * chan + 16, :] = cot_ref[...]

    pl.semaphore_wait(barrier, owners)

    def block_copy(block, kind, target_place):
        return pltpu.make_async_remote_copy(
            src_ref=held.at[block], dst_ref=held.at[block],
            send_sem=send_sem.at[block, kind], recv_sem=recv_sem.at[block],
            device_id=target_place, device_id_type=pl.DeviceIdType.MESH,
        )

    across, sibling = place(w, 1 - n, s), place(w, n, 1 - s)
    last, inner = wide_n - 1, wide_n

    def along(distance, above):
        peer = w + distance if above else w - distance
        kind = lax.rem(peer - w + wide_n, wide_n) - 1
        return block_copy(mine, kind, place(peer, n, s))

    block_copy(mine, last, across).start()
    for distance in range(1, wide_n):

        @pl.when(w + distance < wide_n)
        def _():
            along(distance, True).start()

        @pl.when(w >= distance)
        def _():
            along(distance, False).start()

    block_copy(mine, inner, sibling).start()

    def clear(i, carry):
        x_field[i] = jnp.zeros(x_field.shape[1:], F32)
        g_field[i] = jnp.zeros(g_field.shape[1:], F32)
        return carry

    lax.fori_loop(0, x_field.shape[0], clear, 0)
    taps[...] = jnp.zeros(taps.shape, BF16)
    fetches[3].wait()
    for t in range(27):
        taps[t, 0:chan, 0:chan] = weight_ref[t]

    def slot_mask(block):
        lines = held[block, chan : chan + 16, :].astype(F32)
        slot_of = lines[0:1] * 16.0 + lines[1:2]
        order = lax.broadcasted_iota(jnp.int32, (slot_n, rows), 0).astype(F32)
        return jnp.where(order == slot_of, 1.0, 0.0).astype(BF16)

    def to_slots(block):
        spare = jnp.zeros((LANES - chan, rows), BF16)
        lines_in = jnp.concatenate(
            [
                held[block, 0 : chan + 16, :], spare[16:],
                held[block, chan + 16 : 2 * chan + 16, :], spare,
            ],
            axis=0,
        )
        filled = lax.dot_general(
            slot_mask(block), lines_in, (((1,), (1,)), ((), ())), preferred_element_type=F32
        )
        source = block // sub_n
        slots[block % sub_n, :, source] = filled.astype(BF16).reshape(owners, cap, 2 * LANES)

    row_of = lax.broadcasted_iota(jnp.int32, (16, 2 * LANES), 0)
    lane_of = lax.broadcasted_iota(jnp.int32, (16, 2 * LANES), 1)
    chooser = jnp.where(lane_of == chan + 2, 16.0, jnp.where(lane_of == chan + 3, 1.0, 0.0))
    chooser = jnp.where(row_of == 0, chooser, 0.0).astype(BF16)

    def find_cells(si):
        found = lax.dot_general(
            chooser, slots[si].reshape(owners * slot_n, 2 * LANES), (((1,), (1,)), ((), ())),
            preferred_element_type=F32,
        )
        for o in range(owners):
            cell_rows[si, o] = found[0:8, o * slot_n : (o + 1) * slot_n]

    def cell_mask(block):
        cell_of = cell_rows[block % sub_n, block // sub_n][0:1]
        order = lax.broadcasted_iota(jnp.int32, (cells, slot_n), 0).astype(F32) + 1.0
        return jnp.where(order == cell_of, 1.0, 0.0).astype(BF16)

    def to_field(block):
        rows_in = slots[block % sub_n, block // sub_n].reshape(slot_n, 2 * LANES)
        dense = jnp.dot(cell_mask(block), rows_in, preferred_element_type=F32)
        dense = dense.reshape(EDGE, half, EDGE, 2 * LANES)
        owner = block // sub_n
        at = (
            pl.ds(1 + EDGE * (owner % narrow_n), EDGE),
            pl.ds(1 + half * (block % sub_n), half),
            pl.ds(pl.multiple_of(EDGE + EDGE * (owner // narrow_n), EDGE), EDGE),
        )
        x_field[at] = dense[..., 0:LANES]
        g_field[at] = dense[..., LANES : 2 * LANES]

    to_slots(mine)

    def offset(step):
        distance = (step + 1) // 2
        wi = jnp.where(step % 2 == 1, w - distance, w + distance)
        return wi, jnp.logical_and(wi >= 0, wi < wide_n)

    def arrive(step, carry):
        wi, valid = offset(step)

        @pl.when(jnp.logical_and(valid, jnp.logical_and(step >= 1, step < 2 * wide_n - 1)))
        def _():
            block = number(wi, n, s)
            block_copy(block, last, across).wait_recv()
            block_copy(block, last, across).start()
            block_copy(block, inner, sibling).start()
            to_slots(block)

        wx, there = offset(step - 2)

        @pl.when(jnp.logical_and(there, step >= 2))
        def _():
            block = number(wx, 1 - n, s)
            block_copy(block, last, across).wait_recv()
            block_copy(block, inner, sibling).start()
            to_slots(block)

        return carry

    lax.fori_loop(1, 2 * wide_n + 1, arrive, 0)

    def fields_of(si, begin, end):
        def one(i, carry):
            wi = lax.rem(w + wide_n - 1 + i // narrow_n, wide_n)
            to_field(number(wi, i % narrow_n, si))
            return carry

        lax.fori_loop(begin * narrow_n, end * narrow_n, one, 0, unroll=2)

    close = min(3, wide_n)
    find_cells(s)
    fields_of(s, 0, close)

    def from_sibling(o, carry):
        block = o * sub_n + 1 - s
        block_copy(block, inner, sibling).wait_recv()
        to_slots(block)
        return carry

    lax.fori_loop(0, owners, from_sibling, 0)
    find_cells(1 - s)
    fields_of(1 - s, 0, close)
    mask[...] = cell_mask(mine)

    wide_at = pl.ds(pl.multiple_of(EDGE * w, EDGE), 3 * EDGE)

    def near(i, carry):
        for k in range(half + 2):
            x_line = x_field[EDGE * n + i, half * s + k, wide_at, :]
            g_line = g_field[EDGE * n + i, half * s + k, wide_at, :]
            for j in range(3):
                begin = EDGE - 1 + j
                x_near[j, i, k] = x_line[begin : begin + EDGE].astype(BF16)
                g_near[j, i, k] = g_line[begin : begin + EDGE].astype(BF16)
        return carry

    lax.fori_loop(0, EDGE + 2, near, 0)

    forward[...] = jnp.zeros(forward.shape, F32)
    backward[...] = jnp.zeros(backward.shape, F32)

    def conv(group, carry):
        i, j = group // 3, group % 3
        ahead = jnp.concatenate(
            [x_near[j, pl.ds(i, EDGE), k : k + half].reshape(cells, LANES) for k in range(3)],
            axis=1,
        )
        behind = [
            g_near[2 - j, pl.ds(2 - i, EDGE), 2 - k : 2 - k + half].reshape(cells, LANES)
            for k in range(3)
        ]
        forward[...] += jnp.dot(
            ahead, taps[pl.ds(3 * group, 3)].reshape(3 * LANES, LANES), preferred_element_type=F32
        )
        total = backward[...]
        for k in range(3):
            total += lax.dot_general(
                behind[k], taps[3 * group + k], (((1,), (1,)), ((), ())),
                preferred_element_type=F32,
            )
        backward[...] = total
        return carry

    lax.fori_loop(0, 9, conv, 0)

    reply = jnp.concatenate([forward[...].astype(BF16), backward[...].astype(BF16)], axis=1)
    rows_out = lax.dot_general(
        mask[...], reply, (((0,), (0,)), ((), ())), preferred_element_type=F32
    ).astype(BF16)
    picked[...] = rows_out.reshape(owners, cap, 2 * LANES)

    def reply_copy(delta):
        peer = lax.rem(me + delta, owners)
        return pltpu.make_async_remote_copy(
            src_ref=picked.at[peer], dst_ref=returned.at[me],
            send_sem=reply_send.at[delta], recv_sem=reply_recv.at[delta],
            device_id=place(peer // narrow_n, peer % narrow_n, s),
            device_id_type=pl.DeviceIdType.MESH,
        )

    def reply_arrival(delta):
        peer = lax.rem(me + owners - delta, owners)
        return pltpu.make_async_remote_copy(
            src_ref=picked.at[peer], dst_ref=returned.at[peer],
            send_sem=reply_send.at[delta], recv_sem=reply_recv.at[delta],
            device_id=place(peer // narrow_n, peer % narrow_n, s),
            device_id_type=pl.DeviceIdType.MESH,
        )

    for delta in range(1, owners):
        reply_copy(delta).start()
    returned[me] = picked[me]

    fields_of(s, close, wide_n)
    fields_of(1 - s, close, wide_n)
    begin = mine * shard
    tap0 = begin // chan
    whole = EDGE * wide_n
    terms[...] = jnp.zeros(terms.shape, F32)
    steps = []
    for m in range(3):
        t = jnp.minimum(tap0 + m, 26)
        steps.append((t // 9, t // 3 % 3, t % 3))

    def gather(i, carry):
        right = []
        for a, b, c in steps:
            right.append(
                jnp.concatenate(
                    [
                        x_field[i + a, c + k, pl.ds(EDGE - 1 + b, whole), :].astype(BF16)
                        for k in range(DEPTH)
                    ],
                    axis=0,
                )
            )
        left = jnp.concatenate(
            [g_field[1 + i, 1 + k, EDGE : EDGE + whole, :].astype(BF16) for k in range(DEPTH)],
            axis=0,
        )
        terms[...] += lax.dot_general(
            left, jnp.concatenate(right, axis=1), (((0,), (0,)), ((), ())),
            preferred_element_type=F32,
        )
        return carry

    lax.fori_loop(0, EDGE * narrow_n, gather, 0)
    total_rows = rows * owners * sub_n
    factor = F32(1.0) / jnp.sqrt(F32(total_rows))
    for m in range(3):
        flipped = jnp.transpose(terms[:, m * LANES : (m + 1) * LANES])
        forward[m * chan : (m + 1) * chan, :] = flipped[0:chan] * factor
    wgrad_ref[...] = forward[pl.ds(begin - tap0 * chan, shard), :][:, 0:chan]

    for delta in range(1, owners):
        reply_copy(delta).wait_send()
        reply_arrival(delta).wait_recv()
    for delta in range(1, wide_n):
        block_copy(mine, delta - 1, across).wait_send()
    for wi in range(wide_n):
        block = number(wi, n, s)
        block_copy(block, last, across).wait_send()
        for ni in range(narrow_n):
            block_copy(number(wi, ni, s), inner, sibling).wait_send()

    answer = lax.dot_general(
        returned[...].reshape(slot_n, 2 * LANES), slot_mask(mine), (((0,), (0,)), ((), ())),
        preferred_element_type=F32,
    ).astype(BF16)
    out_ref[...] = answer[0:chan]
    grad_ref[...] = answer[LANES : LANES + chan]


def window_shards(features, cotangent, keys, weight):
    rows, chan = features.shape
    wide_n, narrow_n, sub_n = (lax.axis_size(a) for a in ("wide", "narrow", "sub"))
    owners = wide_n * narrow_n
    cap = 2 * rows // owners
    half = DEPTH // sub_n
    cells = EDGE * EDGE * half
    shard = 27 * chan // (owners * sub_n)
    field = (EDGE * narrow_n + 2, DEPTH + 2, EDGE * wide_n + 2 * EDGE, LANES)
    near = (3, EDGE + 2, half + 2, EDGE, LANES)
    dims = (wide_n, narrow_n, sub_n, rows, chan, cap, shard)
    vmem = pl.BlockSpec(memory_space=pltpu.VMEM)
    out, grad, terms = pl.pallas_call(
        functools.partial(window_kernel, dims),
        out_shape=(
            jax.ShapeDtypeStruct((chan, rows), BF16),
            jax.ShapeDtypeStruct((chan, rows), BF16),
            jax.ShapeDtypeStruct((shard, chan), F32),
        ),
        in_specs=[pl.BlockSpec(memory_space=pltpu.HBM)] * 4,
        out_specs=(vmem,) * 3,
        scratch_shapes=[
            pltpu.VMEM((owners * sub_n, 2 * chan + 16, rows), BF16),
            pltpu.VMEM((sub_n, owners, owners, cap, 2 * LANES), BF16),
            pltpu.VMEM(field, F32),
            pltpu.VMEM(field, F32),
            pltpu.VMEM(near, BF16),
            pltpu.VMEM(near, BF16),
            pltpu.VMEM((27, LANES, LANES), BF16),
            pltpu.VMEM((cells, owners * cap), BF16),
            pltpu.VMEM((cells, LANES), F32),
            pltpu.VMEM((cells, LANES), F32),
            pltpu.VMEM((owners, cap, 2 * LANES), BF16),
            pltpu.VMEM((owners, cap, 2 * LANES), BF16),
            pltpu.VMEM((LANES, 3 * LANES), F32),
            pltpu.VMEM((chan, rows), BF16),
            pltpu.VMEM((chan, rows), BF16),
            pltpu.VMEM((1, rows), jnp.int32),
            pltpu.VMEM((27, chan, chan), BF16),
            pltpu.VMEM((sub_n, owners, 8, owners * cap), F32),
            pltpu.SemaphoreType.DMA((4,)),
            pltpu.SemaphoreType.DMA((owners * sub_n, wide_n + 1)),
            pltpu.SemaphoreType.DMA((owners * sub_n,)),
            pltpu.SemaphoreType.DMA((owners,)),
            pltpu.SemaphoreType.DMA((owners,)),
        ],
        compiler_params=pltpu.CompilerParams(
            collective_id=0, has_side_effects=True, vmem_limit_bytes=63 * 1024 * 1024
        ),
    )(features.T, cotangent.T, keys.reshape(1, rows), weight)
    return out.T, grad.T, terms.reshape(-1)


def extended(array, sides, width):
    for axis, dim in sides:
        size, length = (lax.axis_size(axis), array.shape[dim])
        up = [(i, (i + 1) % size) for i in range(size - 1)]
        down = [(j, i) for i, j in up]
        last = lax.slice_in_dim(array, length - width, length, axis=dim)
        first = lax.slice_in_dim(array, 0, width, axis=dim)
        before = lax.ppermute(last, axis, up)
        after = lax.ppermute(first, axis, down)
        array = jnp.concatenate([before, array, after], axis=dim)
    return array


def brick_pass(padded, weight, chan_count, half_depth):
    fields = padded[..., :chan_count]
    back_field = padded[..., chan_count:]
    centre = back_field[1:-1, 1:-1, 1:-1].reshape(-1, chan_count)
    cell_count = EDGE * EDGE * half_depth
    forward = jnp.zeros((cell_count, chan_count), jnp.float32)
    backward = jnp.zeros((cell_count, chan_count), jnp.float32)
    pieces = []
    for group in range(9):
        step_x = group // 3 - 1
        step_y = group % 3 - 1
        shifted = jnp.concatenate(
            [
                fields[
                    1 + step_x : 1 + step_x + EDGE,
                    1 + step_y : 1 + step_y + EDGE,
                    1 + step_z : 1 + step_z + half_depth,
                ]
                for step_z in (-1, 0, 1)
            ],
            axis=3,
        ).reshape(-1, 3 * chan_count)
        mirrored = jnp.concatenate(
            [
                back_field[
                    1 - step_x : 1 - step_x + EDGE,
                    1 - step_y : 1 - step_y + EDGE,
                    1 - step_z : 1 - step_z + half_depth,
                ]
                for step_z in (-1, 0, 1)
            ],
            axis=3,
        ).reshape(-1, 3 * chan_count)
        tap_block = weight[3 * group : 3 * group + 3]
        forward = forward + jnp.dot(
            shifted,
            tap_block.reshape(3 * chan_count, chan_count),
            preferred_element_type=jnp.float32,
        )
        backward = backward + jnp.dot(
            mirrored,
            jnp.transpose(tap_block, (0, 2, 1)).reshape(3 * chan_count, chan_count),
            preferred_element_type=jnp.float32,
        )
        pieces.append(
            lax.dot_general(
                shifted, centre, (((0,), (0,)), ((), ())), preferred_element_type=jnp.float32
            )
        )
    weight_terms = jnp.concatenate(pieces, axis=0)
    return (forward.astype(jnp.bfloat16), backward.astype(jnp.bfloat16), weight_terms)


def shards(features, cotangent, keys, weight):
    row_count, chan_count = features.shape
    wide_size = lax.axis_size("wide")
    narrow = lax.axis_size("narrow")
    sub_size = lax.axis_size("sub")
    owners = wide_size * narrow
    capacity = 2 * row_count // owners
    slot_count = owners * capacity
    half_depth = DEPTH // sub_size
    cell_count = EDGE * EDGE * half_depth
    target = keys // cell_count // sub_size
    local_cell = keys % cell_count
    columns = jnp.arange(owners, dtype=jnp.int32)
    before = jnp.sum((target[:, None] < columns[None, :]).astype(jnp.int32), axis=0)
    matches = target[:, None] == columns[None, :]
    first_row = jnp.sum(jnp.where(matches, before[None, :], 0), axis=1)
    row_rank = jnp.arange(row_count, dtype=jnp.int32) - first_row
    send_slot = target * capacity + row_rank
    payload = jnp.concatenate([features, cotangent], axis=1)
    outgoing = jnp.zeros((slot_count, 2 * chan_count), jnp.bfloat16).at[send_slot].set(payload)
    placed = jnp.full((slot_count,), -1, jnp.int32).at[send_slot].set(local_cell)
    incoming, arrived = (
        lax.all_to_all(outgoing, ("wide", "narrow"), split_axis=0, concat_axis=0, tiled=True),
        lax.all_to_all(placed, ("wide", "narrow"), split_axis=0, concat_axis=0, tiled=True),
    )
    is_live = arrived >= 0
    position = jnp.where(is_live, arrived, cell_count)
    dense = jnp.zeros((cell_count + 1, 2 * chan_count), jnp.bfloat16).at[position].set(incoming)
    dense = dense[:cell_count].reshape(EDGE, EDGE, half_depth, 2 * chan_count)
    padded = extended(dense, (("wide", 1), ("narrow", 0), ("sub", 2)), 1)
    outputs, gradient, weight_terms = brick_pass(padded, weight, chan_count, half_depth)
    reply = jnp.concatenate([outputs, gradient], axis=1)
    picked = jnp.where(
        is_live[:, None], reply[jnp.where(is_live, arrived, 0)], jnp.zeros((), jnp.bfloat16)
    )
    returned = lax.all_to_all(picked, ("wide", "narrow"), split_axis=0, concat_axis=0, tiled=True)
    answer = returned[send_slot]
    flat_terms = weight_terms.reshape(-1)
    partial_value = lax.psum_scatter(flat_terms, "wide", scatter_dimension=0, tiled=True)
    summed = lax.psum_scatter(partial_value, ("narrow", "sub"), scatter_dimension=0, tiled=True)
    factor = jnp.float32(1.0) / jnp.sqrt(jnp.float32(row_count * owners * sub_size))
    return (answer[:, :chan_count], answer[:, chan_count:], summed * factor)


def solution(mesh):
    placed = (
        P(("groups", "wide", "narrow", "sub"), None),
        P(("groups", "wide", "narrow", "sub"), None),
        P(("groups", "wide", "narrow", "sub")),
        P(),
    )
    sizes = mesh.shape
    gathered = sizes["wide"] * sizes["narrow"] <= 8 and sizes["narrow"] == 2 and sizes["sub"] == 2
    return jax.shard_map(
        window_shards if gathered else shards,
        mesh=mesh,
        in_specs=placed,
        out_specs=(
            P(("groups", "wide", "narrow", "sub"), None),
            P(("groups", "wide", "narrow", "sub"), None),
            P(("groups", "wide", "narrow", "sub")),
        ),
        check_vma=False,
    )
```

```python
import functools

import jax
import jax.numpy as jnp
from jax import lax
from jax.experimental import pallas as pl
from jax.experimental.pallas import tpu as pltpu
from jax.sharding import PartitionSpec as P

EDGE = 16
DEPTH = 4
LANES = 128
F32, BF16 = jnp.float32, jnp.bfloat16


def window_kernel(
    dims, feat_in, cot_in, keys_in, weight_in, out_ref, grad_ref, wgrad_ref,
    held, slots, x_field, g_field, x_near, g_near, taps, mask, forward, backward,
    picked, returned, terms, feat_ref, cot_ref, keys_ref, weight_ref, cell_rows, fetch_sem, send_sem, recv_sem, reply_send, reply_recv,
):
    wide_n, narrow_n, sub_n, rows, chan, cap, shard = dims
    owners = wide_n * narrow_n
    slot_n = owners * cap
    half = DEPTH // sub_n
    cells = EDGE * EDGE * half
    w, n, s = lax.axis_index("wide"), lax.axis_index("narrow"), lax.axis_index("sub")
    me = w * narrow_n + n

    def number(wi, ni, si):
        return (wi * narrow_n + ni) * sub_n + si

    def place(wi, ni, si):
        return {"wide": wi, "narrow": ni, "sub": si}

    fetches = [
        pltpu.make_async_copy(source, goal, fetch_sem.at[i])
        for i, (source, goal) in enumerate(
            ((keys_in, keys_ref), (feat_in, feat_ref), (cot_in, cot_ref), (weight_in, weight_ref))
        )
    ]
    for fetch in fetches:
        fetch.start()

    barrier = pltpu.get_barrier_semaphore()
    for delta in range(1, owners):
        peer = lax.rem(me + delta, owners)
        pl.semaphore_signal(
            barrier, inc=1, device_id=place(peer // narrow_n, peer % narrow_n, s),
            device_id_type=pl.DeviceIdType.MESH,
        )
    pl.semaphore_signal(
        barrier, inc=1, device_id=place(w, n, 1 - s), device_id_type=pl.DeviceIdType.MESH
    )

    fetches[0].wait()
    keys = keys_ref[...]
    target = lax.shift_right_logical(keys, (cells * sub_n).bit_length() - 1)
    local = keys & (cells - 1)
    cell = (local >> 5) * 32 + (local & 1) * EDGE + ((local >> 1) & (EDGE - 1))
    first = jnp.zeros_like(keys)
    for o in range(1, owners):
        before = jnp.sum((target < o).astype(F32), axis=1, keepdims=True).astype(jnp.int32)
        first = jnp.where(target == o, before, first)
    slot = target * cap + lax.broadcasted_iota(jnp.int32, keys.shape, 1) - first
    cell1 = cell + 1
    line = lax.broadcasted_iota(jnp.int32, (16, rows), 0)
    digits = jnp.where(line == 0, slot >> 4, 0)
    digits = jnp.where(line == 1, slot & 15, digits)
    digits = jnp.where(line == 2, cell1 >> 4, digits)
    digits = jnp.where(line == 3, cell1 & 15, digits)
    digits = digits.astype(F32).astype(BF16)
    fetches[1].wait()
    fetches[2].wait()
    mine = number(w, n, s)
    held[mine, 0:chan, :] = feat_ref[...]
    held[mine, chan : chan + 16, :] = digits
    held[mine, chan + 16 : 2 * chan + 16, :] = cot_ref[...]

    pl.semaphore_wait(barrier, owners)

    def block_copy(block, kind, target_place):
        return pltpu.make_async_remote_copy(
            src_ref=held.at[block], dst_ref=held.at[block],
            send_sem=send_sem.at[block, kind], recv_sem=recv_sem.at[block],
            device_id=target_place, device_id_type=pl.DeviceIdType.MESH,
        )

    across, sibling = place(w, 1 - n, s), place(w, n, 1 - s)
    last, inner = wide_n - 1, wide_n

    def along(distance, above):
        peer = w + distance if above else w - distance
        kind = lax.rem(peer - w + wide_n, wide_n) - 1
        return block_copy(mine, kind, place(peer, n, s))

    block_copy(mine, last, across).start()
    for distance in range(1, wide_n):

        @pl.when(w + distance < wide_n)
        def _():
            along(distance, True).start()

        @pl.when(w >= distance)
        def _():
            along(distance, False).start()

    block_copy(mine, inner, sibling).start()

    def clear(i, carry):
        x_field[i] = jnp.zeros(x_field.shape[1:], F32)
        g_field[i] = jnp.zeros(g_field.shape[1:], F32)
        return carry

    lax.fori_loop(0, x_field.shape[0], clear, 0)
    taps[...] = jnp.zeros(taps.shape, BF16)
    fetches[3].wait()
    for t in range(27):
        taps[t, 0:chan, 0:chan] = weight_ref[t]

    def slot_mask(block):
        lines = held[block, chan : chan + 16, :].astype(F32)
        slot_of = lines[0:1] * 16.0 + lines[1:2]
        order = lax.broadcasted_iota(jnp.int32, (slot_n, rows), 0).astype(F32)
        return jnp.where(order == slot_of, 1.0, 0.0).astype(BF16)

    def to_slots(block):
        spare = jnp.zeros((LANES - chan, rows), BF16)
        lines_in = jnp.concatenate(
            [
                held[block, 0 : chan + 16, :], spare[16:],
                held[block, chan + 16 : 2 * chan + 16, :], spare,
            ],
            axis=0,
        )
        filled = lax.dot_general(
            slot_mask(block), lines_in, (((1,), (1,)), ((), ())), preferred_element_type=F32
        )
        source = block // sub_n
        slots[block % sub_n, :, source] = filled.astype(BF16).reshape(owners, cap, 2 * LANES)

    row_of = lax.broadcasted_iota(jnp.int32, (16, 2 * LANES), 0)
    lane_of = lax.broadcasted_iota(jnp.int32, (16, 2 * LANES), 1)
    chooser = jnp.where(lane_of == chan + 2, 16.0, jnp.where(lane_of == chan + 3, 1.0, 0.0))
    chooser = jnp.where(row_of == 0, chooser, 0.0).astype(BF16)

    def find_cells(si):
        found = lax.dot_general(
            chooser, slots[si].reshape(owners * slot_n, 2 * LANES), (((1,), (1,)), ((), ())),
            preferred_element_type=F32,
        )
        for o in range(owners):
            cell_rows[si, o] = found[0:8, o * slot_n : (o + 1) * slot_n]

    def cell_mask(block):
        cell_of = cell_rows[block % sub_n, block // sub_n][0:1]
        order = lax.broadcasted_iota(jnp.int32, (cells, slot_n), 0).astype(F32) + 1.0
        return jnp.where(order == cell_of, 1.0, 0.0).astype(BF16)

    def to_field(block):
        rows_in = slots[block % sub_n, block // sub_n].reshape(slot_n, 2 * LANES)
        dense = jnp.dot(cell_mask(block), rows_in, preferred_element_type=F32)
        dense = dense.reshape(EDGE, half, EDGE, 2 * LANES)
        owner = block // sub_n
        at = (
            pl.ds(1 + EDGE * (owner % narrow_n), EDGE),
            pl.ds(1 + half * (block % sub_n), half),
            pl.ds(pl.multiple_of(EDGE + EDGE * (owner // narrow_n), EDGE), EDGE),
        )
        x_field[at] = dense[..., 0:LANES]
        g_field[at] = dense[..., LANES : 2 * LANES]

    to_slots(mine)

    def offset(step):
        distance = (step + 1) // 2
        wi = jnp.where(step % 2 == 1, w - distance, w + distance)
        return wi, jnp.logical_and(wi >= 0, wi < wide_n)

    def arrive(step, carry):
        wi, valid = offset(step)

        @pl.when(jnp.logical_and(valid, jnp.logical_and(step >= 1, step < 2 * wide_n - 1)))
        def _():
            block = number(wi, n, s)
            block_copy(block, last, across).wait_recv()
            block_copy(block, last, across).start()
            block_copy(block, inner, sibling).start()
            to_slots(block)

        wx, there = offset(step - 2)

        @pl.when(jnp.logical_and(there, step >= 2))
        def _():
            block = number(wx, 1 - n, s)
            block_copy(block, last, across).wait_recv()
            block_copy(block, inner, sibling).start()
            to_slots(block)

        return carry

    lax.fori_loop(1, 2 * wide_n + 1, arrive, 0)

    def fields_of(si, begin, end):
        def one(i, carry):
            wi = lax.rem(w + wide_n - 1 + i // narrow_n, wide_n)
            to_field(number(wi, i % narrow_n, si))
            return carry

        lax.fori_loop(begin * narrow_n, end * narrow_n, one, 0, unroll=True)

    close = min(3, wide_n)
    find_cells(s)
    fields_of(s, 0, close)

    def from_sibling(o, carry):
        block = o * sub_n + 1 - s
        block_copy(block, inner, sibling).wait_recv()
        to_slots(block)
        return carry

    lax.fori_loop(0, owners, from_sibling, 0, unroll=2)
    find_cells(1 - s)
    fields_of(1 - s, 0, close)
    mask[...] = cell_mask(mine)

    wide_at = pl.ds(pl.multiple_of(EDGE * w, EDGE), 3 * EDGE)

    def near(i, carry):
        for k in range(half + 2):
            x_line = x_field[EDGE * n + i, half * s + k, wide_at, :]
            g_line = g_field[EDGE * n + i, half * s + k, wide_at, :]
            for j in range(3):
                begin = EDGE - 1 + j
                x_near[j, i, k] = x_line[begin : begin + EDGE].astype(BF16)
                g_near[j, i, k] = g_line[begin : begin + EDGE].astype(BF16)
        return carry

    lax.fori_loop(0, EDGE + 2, near, 0, unroll=3)

    forward[...] = jnp.zeros(forward.shape, F32)
    backward[...] = jnp.zeros(backward.shape, F32)

    def conv(group, carry):
        i, j = group // 3, group % 3
        ahead = jnp.concatenate(
            [x_near[j, pl.ds(i, EDGE), k : k + half].reshape(cells, LANES) for k in range(3)],
            axis=1,
        )
        behind = [
            g_near[2 - j, pl.ds(2 - i, EDGE), 2 - k : 2 - k + half].reshape(cells, LANES)
            for k in range(3)
        ]
        forward[...] += jnp.dot(
            ahead, taps[pl.ds(3 * group, 3)].reshape(3 * LANES, LANES), preferred_element_type=F32
        )
        total = backward[...]
        for k in range(3):
            total += lax.dot_general(
                behind[k], taps[3 * group + k], (((1,), (1,)), ((), ())),
                preferred_element_type=F32,
            )
        backward[...] = total
        return carry

    lax.fori_loop(0, 9, conv, 0, unroll=3)

    reply = jnp.concatenate([forward[...].astype(BF16), backward[...].astype(BF16)], axis=1)
    rows_out = lax.dot_general(
        mask[...], reply, (((0,), (0,)), ((), ())), preferred_element_type=F32
    ).astype(BF16)
    picked[...] = rows_out.reshape(owners, cap, 2 * LANES)

    def reply_copy(delta):
        peer = lax.rem(me + delta, owners)
        return pltpu.make_async_remote_copy(
            src_ref=picked.at[peer], dst_ref=returned.at[me],
            send_sem=reply_send.at[delta], recv_sem=reply_recv.at[delta],
            device_id=place(peer // narrow_n, peer % narrow_n, s),
            device_id_type=pl.DeviceIdType.MESH,
        )

    def reply_arrival(delta):
        peer = lax.rem(me + owners - delta, owners)
        return pltpu.make_async_remote_copy(
            src_ref=picked.at[peer], dst_ref=returned.at[peer],
            send_sem=reply_send.at[delta], recv_sem=reply_recv.at[delta],
            device_id=place(peer // narrow_n, peer % narrow_n, s),
            device_id_type=pl.DeviceIdType.MESH,
        )

    for delta in range(1, owners):
        reply_copy(delta).start()
    returned[me] = picked[me]

    fields_of(s, close, wide_n)
    fields_of(1 - s, close, wide_n)
    begin = mine * shard
    tap0 = begin // chan
    whole = EDGE * wide_n
    terms[...] = jnp.zeros(terms.shape, F32)
    steps = []
    for m in range(3):
        t = jnp.minimum(tap0 + m, 26)
        steps.append((t // 9, t // 3 % 3, t % 3))

    def gather(i, carry):
        right = []
        for a, b, c in steps:
            right.append(
                jnp.concatenate(
                    [
                        x_field[i + a, c + k, pl.ds(EDGE - 1 + b, whole), :].astype(BF16)
                        for k in range(DEPTH)
                    ],
                    axis=0,
                )
            )
        left = jnp.concatenate(
            [g_field[1 + i, 1 + k, EDGE : EDGE + whole, :].astype(BF16) for k in range(DEPTH)],
            axis=0,
        )
        terms[...] += lax.dot_general(
            left, jnp.concatenate(right, axis=1), (((0,), (0,)), ((), ())),
            preferred_element_type=F32,
        )
        return carry

    lax.fori_loop(0, EDGE * narrow_n, gather, 0, unroll=4)
    total_rows = rows * owners * sub_n
    factor = F32(1.0) / jnp.sqrt(F32(total_rows))
    for m in range(3):
        flipped = jnp.transpose(terms[:, m * LANES : (m + 1) * LANES])
        forward[m * chan : (m + 1) * chan, :] = flipped[0:chan] * factor
    wgrad_ref[...] = forward[pl.ds(begin - tap0 * chan, shard), :][:, 0:chan]

    for delta in range(1, owners):
        reply_copy(delta).wait_send()
        reply_arrival(delta).wait_recv()
    for delta in range(1, wide_n):
        block_copy(mine, delta - 1, across).wait_send()
    for wi in range(wide_n):
        block = number(wi, n, s)
        block_copy(block, last, across).wait_send()
        for ni in range(narrow_n):
            block_copy(number(wi, ni, s), inner, sibling).wait_send()

    answer = lax.dot_general(
        returned[...].reshape(slot_n, 2 * LANES), slot_mask(mine), (((0,), (0,)), ((), ())),
        preferred_element_type=F32,
    ).astype(BF16)
    out_ref[...] = answer[0:chan]
    grad_ref[...] = answer[LANES : LANES + chan]


def window_shards(features, cotangent, keys, weight):
    rows, chan = features.shape
    wide_n, narrow_n, sub_n = (lax.axis_size(a) for a in ("wide", "narrow", "sub"))
    owners = wide_n * narrow_n
    cap = 2 * rows // owners
    half = DEPTH // sub_n
    cells = EDGE * EDGE * half
    shard = 27 * chan // (owners * sub_n)
    field = (EDGE * narrow_n + 2, DEPTH + 2, EDGE * wide_n + 2 * EDGE, LANES)
    near = (3, EDGE + 2, half + 2, EDGE, LANES)
    dims = (wide_n, narrow_n, sub_n, rows, chan, cap, shard)
    vmem = pl.BlockSpec(memory_space=pltpu.VMEM)
    out, grad, terms = pl.pallas_call(
        functools.partial(window_kernel, dims),
        out_shape=(
            jax.ShapeDtypeStruct((chan, rows), BF16),
            jax.ShapeDtypeStruct((chan, rows), BF16),
            jax.ShapeDtypeStruct((shard, chan), F32),
        ),
        in_specs=[pl.BlockSpec(memory_space=pltpu.HBM)] * 4,
        out_specs=(vmem,) * 3,
        scratch_shapes=[
            pltpu.VMEM((owners * sub_n, 2 * chan + 16, rows), BF16),
            pltpu.VMEM((sub_n, owners, owners, cap, 2 * LANES), BF16),
            pltpu.VMEM(field, F32),
            pltpu.VMEM(field, F32),
            pltpu.VMEM(near, BF16),
            pltpu.VMEM(near, BF16),
            pltpu.VMEM((27, LANES, LANES), BF16),
            pltpu.VMEM((cells, owners * cap), BF16),
            pltpu.VMEM((cells, LANES), F32),
            pltpu.VMEM((cells, LANES), F32),
            pltpu.VMEM((owners, cap, 2 * LANES), BF16),
            pltpu.VMEM((owners, cap, 2 * LANES), BF16),
            pltpu.VMEM((LANES, 3 * LANES), F32),
            pltpu.VMEM((chan, rows), BF16),
            pltpu.VMEM((chan, rows), BF16),
            pltpu.VMEM((1, rows), jnp.int32),
            pltpu.VMEM((27, chan, chan), BF16),
            pltpu.VMEM((sub_n, owners, 8, owners * cap), F32),
            pltpu.SemaphoreType.DMA((4,)),
            pltpu.SemaphoreType.DMA((owners * sub_n, wide_n + 1)),
            pltpu.SemaphoreType.DMA((owners * sub_n,)),
            pltpu.SemaphoreType.DMA((owners,)),
            pltpu.SemaphoreType.DMA((owners,)),
        ],
        compiler_params=pltpu.CompilerParams(
            collective_id=0, has_side_effects=True, vmem_limit_bytes=63 * 1024 * 1024
        ),
    )(features.T, cotangent.T, keys.reshape(1, rows), weight)
    return out.T, grad.T, terms.reshape(-1)


def extended(array, sides, width):
    for axis, dim in sides:
        size, length = (lax.axis_size(axis), array.shape[dim])
        up = [(i, (i + 1) % size) for i in range(size - 1)]
        down = [(j, i) for i, j in up]
        last = lax.slice_in_dim(array, length - width, length, axis=dim)
        first = lax.slice_in_dim(array, 0, width, axis=dim)
        before = lax.ppermute(last, axis, up)
        after = lax.ppermute(first, axis, down)
        array = jnp.concatenate([before, array, after], axis=dim)
    return array


def brick_pass(padded, weight, chan_count, half_depth):
    fields = padded[..., :chan_count]
    back_field = padded[..., chan_count:]
    centre = back_field[1:-1, 1:-1, 1:-1].reshape(-1, chan_count)
    cell_count = EDGE * EDGE * half_depth
    forward = jnp.zeros((cell_count, chan_count), jnp.float32)
    backward = jnp.zeros((cell_count, chan_count), jnp.float32)
    pieces = []
    for group in range(9):
        step_x = group // 3 - 1
        step_y = group % 3 - 1
        shifted = jnp.concatenate(
            [
                fields[
                    1 + step_x : 1 + step_x + EDGE,
                    1 + step_y : 1 + step_y + EDGE,
                    1 + step_z : 1 + step_z + half_depth,
                ]
                for step_z in (-1, 0, 1)
            ],
            axis=3,
        ).reshape(-1, 3 * chan_count)
        mirrored = jnp.concatenate(
            [
                back_field[
                    1 - step_x : 1 - step_x + EDGE,
                    1 - step_y : 1 - step_y + EDGE,
                    1 - step_z : 1 - step_z + half_depth,
                ]
                for step_z in (-1, 0, 1)
            ],
            axis=3,
        ).reshape(-1, 3 * chan_count)
        tap_block = weight[3 * group : 3 * group + 3]
        forward = forward + jnp.dot(
            shifted,
            tap_block.reshape(3 * chan_count, chan_count),
            preferred_element_type=jnp.float32,
        )
        backward = backward + jnp.dot(
            mirrored,
            jnp.transpose(tap_block, (0, 2, 1)).reshape(3 * chan_count, chan_count),
            preferred_element_type=jnp.float32,
        )
        pieces.append(
            lax.dot_general(
                shifted, centre, (((0,), (0,)), ((), ())), preferred_element_type=jnp.float32
            )
        )
    weight_terms = jnp.concatenate(pieces, axis=0)
    return (forward.astype(jnp.bfloat16), backward.astype(jnp.bfloat16), weight_terms)


def shards(features, cotangent, keys, weight):
    row_count, chan_count = features.shape
    wide_size = lax.axis_size("wide")
    narrow = lax.axis_size("narrow")
    sub_size = lax.axis_size("sub")
    owners = wide_size * narrow
    capacity = 2 * row_count // owners
    slot_count = owners * capacity
    half_depth = DEPTH // sub_size
    cell_count = EDGE * EDGE * half_depth
    target = keys // cell_count // sub_size
    local_cell = keys % cell_count
    columns = jnp.arange(owners, dtype=jnp.int32)
    before = jnp.sum((target[:, None] < columns[None, :]).astype(jnp.int32), axis=0)
    matches = target[:, None] == columns[None, :]
    first_row = jnp.sum(jnp.where(matches, before[None, :], 0), axis=1)
    row_rank = jnp.arange(row_count, dtype=jnp.int32) - first_row
    send_slot = target * capacity + row_rank
    payload = jnp.concatenate([features, cotangent], axis=1)
    outgoing = jnp.zeros((slot_count, 2 * chan_count), jnp.bfloat16).at[send_slot].set(payload)
    placed = jnp.full((slot_count,), -1, jnp.int32).at[send_slot].set(local_cell)
    incoming, arrived = (
        lax.all_to_all(outgoing, ("wide", "narrow"), split_axis=0, concat_axis=0, tiled=True),
        lax.all_to_all(placed, ("wide", "narrow"), split_axis=0, concat_axis=0, tiled=True),
    )
    is_live = arrived >= 0
    position = jnp.where(is_live, arrived, cell_count)
    dense = jnp.zeros((cell_count + 1, 2 * chan_count), jnp.bfloat16).at[position].set(incoming)
    dense = dense[:cell_count].reshape(EDGE, EDGE, half_depth, 2 * chan_count)
    padded = extended(dense, (("wide", 1), ("narrow", 0), ("sub", 2)), 1)
    outputs, gradient, weight_terms = brick_pass(padded, weight, chan_count, half_depth)
    reply = jnp.concatenate([outputs, gradient], axis=1)
    picked = jnp.where(
        is_live[:, None], reply[jnp.where(is_live, arrived, 0)], jnp.zeros((), jnp.bfloat16)
    )
    returned = lax.all_to_all(picked, ("wide", "narrow"), split_axis=0, concat_axis=0, tiled=True)
    answer = returned[send_slot]
    flat_terms = weight_terms.reshape(-1)
    partial_value = lax.psum_scatter(flat_terms, "wide", scatter_dimension=0, tiled=True)
    summed = lax.psum_scatter(partial_value, ("narrow", "sub"), scatter_dimension=0, tiled=True)
    factor = jnp.float32(1.0) / jnp.sqrt(jnp.float32(row_count * owners * sub_size))
    return (answer[:, :chan_count], answer[:, chan_count:], summed * factor)


def solution(mesh):
    placed = (
        P(("groups", "wide", "narrow", "sub"), None),
        P(("groups", "wide", "narrow", "sub"), None),
        P(("groups", "wide", "narrow", "sub")),
        P(),
    )
    sizes = mesh.shape
    gathered = sizes["wide"] * sizes["narrow"] <= 8 and sizes["narrow"] == 2 and sizes["sub"] == 2
    return jax.shard_map(
        window_shards if gathered else shards,
        mesh=mesh,
        in_specs=placed,
        out_specs=(
            P(("groups", "wide", "narrow", "sub"), None),
            P(("groups", "wide", "narrow", "sub"), None),
            P(("groups", "wide", "narrow", "sub")),
        ),
        check_vma=False,
    )
```
